512 devices in a mesh: dp: 32 (over z_hi, x, core), tensor: 16 (over z_lo, y).
Axes of the slice: x: 4, y: 4, z: 16 (z_hi: 4, z_lo: 4; z = z_hi * 4 + z_lo), core: 2. Of those that a mesh axis runs over, the one named last changes fastest.
Arguments:
- queries: bfloat16 [4096, 4096], P('dp', 'tensor'), may hold values from -150 to 150
- keys: bfloat16 [4096, 1024], P('dp'), may hold values from -6 to 6
- values: bfloat16 [4096, 1024], P('dp'), may hold values from -6 to 6
- doc_start: int32 [4096], P('dp'), may hold values from 0 to 4094, as said below
- out_weight: bfloat16 [4096, 8192], P('tensor', 'dp'), may hold values from -0.09375 to 0.09375
- residual: bfloat16 [4096, 8192], P('dp', 'tensor'), may hold values from -60 to 60
- gain: bfloat16 [8192], P('tensor'), may hold values from 0.5 to 1.5
- cotangent: bfloat16 [4096, 8192], P('dp', 'tensor'), may hold values from -6 to 6
Outputs:
- mixed: bfloat16 [4096, 8192], P('dp', 'tensor')
- normed: bfloat16 [4096, 8192], P('dp', 'tensor')
- grad_weight: bfloat16 [4096, 8192], P('tensor', 'dp')
- grad_heads: bfloat16 [4096, 4096], P('dp', 'tensor')
The draws below stay inside these ranges and needn't reach their ends.
Inputs may be any that keep to these rules, and one draw needn't show every extreme that they name: doc_start[i] <= i, doc_start[i] lies in the same block of 128 rows as i, and equals i or doc_start[i - 1]; the first row of each block starts a document.
All inputs are finite; a program needn't handle non-finite values.
Results may differ from the reference program's by a relative error of at most 0.024.
Values may be sent and summed in bfloat16 or wider, within the bound.
A program may use at most 64 MiB of HBM per device.

```python
import math
import jax
import jax.numpy as jnp
from jax import lax

D = 8192
HD = 128
KV_HEADS = 8
TOK_DEV = 128
HEADS = 32
TOKENS = 4096
N_DP = 32


def shared_keys(key):
    raw = jax.random.normal(jax.random.fold_in(key, 101), (TOKENS, KV_HEADS * HD), jnp.float32)
    return jnp.clip(raw, -6.0, 6.0)


def draw_keys(key, part):
    base = shared_keys(key)
    return base.astype(jnp.bfloat16)


def draw_queries(key, part):
    key = jax.random.fold_in(key, 7)
    raw = jnp.clip(jax.random.normal(key, (TOKENS, HEADS, HD), jnp.float32), -6.0, 6.0)
    return raw.reshape(TOKENS, HEADS * HD).astype(jnp.bfloat16)


def draw_doc_start(key, part):
    key = jax.random.fold_in(key, 5)
    marks = jax.random.randint(key, (TOKENS,), 0, 16)
    position = jnp.arange(TOKENS, dtype=jnp.int32)
    random_begin = (marks == 0) & (position != TOKENS - 1)
    begins = random_begin | (position % TOK_DEV == 0) | (position == TOKENS - 2)
    marked = jnp.where(begins, position, 0)
    return lax.cummax(marked).astype(jnp.int32)


def draw_residual(key, part):
    key = jax.random.fold_in(key, 11)
    first, second = jax.random.split(key)
    columns = jnp.arange(D, dtype=jnp.float32) / D
    base = jnp.clip(jax.random.normal(first, (TOKENS, D), jnp.float32), -6.0, 6.0)
    column_scale = 3.0 ** columns
    row_scale = 10.0 ** jax.random.uniform(second, (TOKENS, 1), jnp.float32)
    return (0.3 * base * column_scale[None, :] * row_scale).astype(jnp.bfloat16)


def with_spikes(values, own_key, source, target, parts, factor):
    def block_of(dim):
        return (jnp.arange(values.shape[dim]) // (values.shape[dim] // parts)).reshape((-1,) + (1,) * (values.ndim - 1 - dim))

    near = jax.random.permutation(own_key, parts)[block_of(target)]
    other_side = (block_of(target) + parts // 2) % parts
    return jnp.where((block_of(source) == near) | (block_of(source) == other_side), factor * values, values)


def steps_of(stream_key, shape, cuts, least, top_value):
    level, own = 1.0, jax.random.fold_in(stream_key, 6)
    for dim, parts in cuts:
        draws = jnp.exp(jax.random.uniform(jax.random.fold_in(own, dim), (parts,), jnp.float32, least / len(cuts), top_value / len(cuts)))
        level = level * jnp.repeat(draws, shape[dim] // parts).reshape([-1 if axis == dim else 1 for axis in range(len(shape))])
    return level


def centred(own_key, shape, deviation, reach, pieces=(), kind=jnp.bfloat16):
    array = deviation * jax.random.normal(own_key, shape, jnp.float32)
    if pieces:
        array = array * steps_of(own_key, shape, pieces, -0.22, 0.18)
    return jnp.clip(array, -reach, reach).astype(kind)


def noise_with(key, dims, scale, limit, shards, heavy, held_as=jnp.bfloat16):
    values = scale * jax.random.normal(key, dims, jnp.float32)
    if shards:
        values = values * steps_of(key, dims, shards, -0.22, 0.18)
    return jnp.clip(with_spikes(values, jax.random.fold_in(key, 3), *heavy), -limit, limit).astype(held_as)


def setup_inputs(seed: int = 0) -> dict:
    seeds = jax.random.split(jax.random.key(seed), 9)
    queries = draw_queries(jax.random.fold_in(seeds[8], 71), 0)
    keys = draw_keys(jax.random.fold_in(seeds[8], 71), 0)
    values = centred(seeds[2], (TOKENS, KV_HEADS * HD), 1.0, 6.0, ((0, 32),))
    doc_start = draw_doc_start(jax.random.fold_in(seeds[8], 71), 0)
    out_weight = centred(seeds[4], (HEADS * HD, D), (HEADS * HD) ** -0.5, 0.09375, ((0, 16), (1, 32)))
    residual = draw_residual(jax.random.fold_in(seeds[8], 71), 0)
    gain = jnp.clip(1.0 + 0.1 * jax.random.normal(seeds[6], (D,), jnp.float32), 0.5, 1.5).astype(jnp.bfloat16)
    cotangent = noise_with(seeds[7], (TOKENS, D), 1.0, 6.0, ((0, 32), (1, 16)), (0, 1, 32, 2.75))
    return {"queries": queries, "keys": keys, "values": values, "doc_start": doc_start, "out_weight": out_weight, "residual": residual, "gain": gain, "cotangent": cotangent}


def reference(queries, keys, values, doc_start, out_weight, residual, gain, cotangent):
    group_size = HEADS // KV_HEADS
    owner = jnp.arange(HEADS) // group_size
    query_blocks = queries.reshape(N_DP, TOK_DEV, HEADS, HD)
    key_blocks = keys.reshape(N_DP, TOK_DEV, KV_HEADS, HD)[:, :, owner, :]
    value_blocks = values.reshape(N_DP, TOK_DEV, KV_HEADS, HD)[:, :, owner, :]
    start_blocks = doc_start.reshape(N_DP, TOK_DEV)
    bases = jnp.arange(N_DP, dtype=jnp.int32) * TOK_DEV

    def sample(args):
        query_rows, key_rows, value_rows, starts, base = args
        scores = jnp.einsum('ihd,jhd->hij', query_rows.astype(jnp.float32), key_rows.astype(jnp.float32)) / math.sqrt(HD)
        position = jnp.arange(TOK_DEV, dtype=jnp.int32)
        allowed = (position[None, :] >= (starts - base)[:, None]) & (position[None, :] <= position[:, None])
        scores = jnp.where(allowed[None], scores, -1e+30)
        top = lax.optimization_barrier(jnp.max(scores, axis=-1, keepdims=True))
        weights = jnp.where(allowed[None], jnp.exp(scores - top), 0.0)
        probs = (weights / lax.optimization_barrier(jnp.sum(weights, axis=-1, keepdims=True))).astype(jnp.bfloat16)
        result = jnp.einsum('hij,jhd->ihd', probs.astype(jnp.float32), value_rows.astype(jnp.float32))
        return result.astype(jnp.bfloat16)
    heads_out = lax.map(sample, (query_blocks, key_blocks, value_blocks, start_blocks, bases))
    heads_out = heads_out.reshape(TOKENS, HEADS * HD)
    projected = jnp.dot(heads_out, out_weight, preferred_element_type=jnp.float32)
    stream = residual.astype(jnp.float32) + projected
    mixed = stream.astype(jnp.bfloat16)
    mean_square = lax.optimization_barrier(jnp.mean(stream * stream, axis=1, keepdims=True))
    normed = (stream * lax.rsqrt(mean_square + 1e-05) * gain.astype(jnp.float32)).astype(jnp.bfloat16)
    out_blocks = heads_out.reshape(N_DP, TOK_DEV, HEADS * HD)
    cot_blocks = cotangent.reshape(N_DP, TOK_DEV, D)

    def accumulate(total, pair):
        block_out, block_cot = pair
        term = jnp.dot(block_out.T, block_cot, preferred_element_type=jnp.float32).astype(jnp.bfloat16)
        term = lax.optimization_barrier(term).astype(jnp.float32)
        return (total + term, None)
    summed, unused = lax.scan(accumulate, jnp.zeros((HEADS * HD, D), jnp.float32), (out_blocks, cot_blocks))
    grad_weight = summed.astype(jnp.bfloat16)
    grad_heads = jnp.dot(cotangent, out_weight.T, preferred_element_type=jnp.float32).astype(jnp.bfloat16)
    return (mixed, normed, grad_weight, grad_heads)
```

```python
import functools
import math

import jax
import jax.numpy as jnp
from jax import lax
from jax.experimental import pallas as pl
from jax.experimental.pallas import tpu as pltpu
from jax.sharding import PartitionSpec as P

HD = 128
EPS = 1e-05
D_MODEL = 8192
MESH = pl.DeviceIdType.MESH
BF16 = jnp.bfloat16
F32 = jnp.float32
N_COPIES = 128


def kernel(
    queries,
    keys,
    values,
    starts_ref,
    weight,
    residual,
    gain,
    cot,
    mixed,
    normed,
    grad_weight,
    grad_heads,
    ho,
    ct,
    pp,
    p_tr,
    p_in,
    s_y,
    z_in,
    q_sum,
    t_in,
    gp,
    g_in,
    gs,
    gx_tr,
    gx_in,
    gh,
    gz_tr,
    gz_in,
    stream,
    sq,
    acc,
    ssem,
    rsem,
):
    dp, tensor = lax.axis_index("dp"), lax.axis_index("tensor")
    zh, x, c = dp // 8, (dp // 2) % 4, dp % 2
    zl, y = tensor // 4, tensor % 4

    def dev(zh_, x_, c_, zl_, y_):
        return ((zh_ * 4 + x_) * 2 + c_, zl_ * 4 + y_)

    def plus(a, k):
        return (a + k) % 4

    y_dev = {k: dev(zh, x, c, zl, plus(y, k)) for k in (1, 2, 3)}
    zl_dev = {k: dev(zh, x, c, plus(zl, k), y) for k in (1, 2, 3)}
    x_dev = {k: dev(zh, plus(x, k), c, zl, y) for k in (1, 3)}
    zh_dev = {k: dev(plus(zh, k), x, c, zl, y) for k in (1, 3)}
    sibling = dev(zh, x, 1 - c, zl, y)
    t_same, t_other = dev(zl, y, c, zh, x), dev(zl, y, 1 - c, zh, x)
    off_diagonal = (zh != zl) | (x != y)
    on_diagonal = (zh == zl) & (x == y)

    barrier = pltpu.get_barrier_semaphore()
    partners = [*y_dev.values(), *zl_dev.values(), *x_dev.values(), *zh_dev.values(), sibling]
    for partner in partners:
        pl.semaphore_signal(barrier, inc=1, device_id=partner, device_id_type=MESH)

    @pl.when(off_diagonal)
    def _():
        for partner in (t_same, t_other):
            pl.semaphore_signal(barrier, inc=1, device_id=partner, device_id_type=MESH)
        pl.semaphore_wait(barrier, len(partners) + 2)

    @pl.when(on_diagonal)
    def _():
        pl.semaphore_wait(barrier, len(partners))

    sent = []
    used = [0]

    def copy(src, dst, device):
        index = used[0]
        used[0] += 1
        return pltpu.make_async_remote_copy(
            src_ref=src,
            dst_ref=dst,
            send_sem=ssem.at[index],
            recv_sem=rsem.at[index],
            device_id=device,
            device_id_type=MESH,
        )

    def send(src, dst, device):
        made = copy(src, dst, device)
        made.start()
        sent.append(made)
        return made

    def transposed(own_src, other_src, dst):
        other = send(other_src, dst, t_other)
        same = copy(own_src, dst, t_same)

        @pl.when(off_diagonal)
        def _():
            same.start()

        @pl.when(on_diagonal)
        def _():
            dst[...] = own_src[...]

        def wait():
            other.wait_recv()

            @pl.when(off_diagonal)
            def _():
                same.wait()

        return wait

    class Gather:
        def __init__(self, slot, half, me, right, left):
            self.half, self.me, self.right, self.left = half, me, right, left
            self.to_right = send(slot(me), slot(me), right)
            self.to_left = send(slot(me), slot(me), left)

        def forward(self):
            self.to_right.wait_recv()
            half = self.half(plus(self.me, 3), 0)
            self.on_right = send(half, half, self.right)
            self.to_left.wait_recv()
            half = self.half(plus(self.me, 1), 1)
            self.on_left = send(half, half, self.left)

        def finish(self):
            self.on_right.wait_recv()
            self.on_left.wait_recv()

    class Reduce:
        def __init__(self, half, tr, arrived, me, right, left):
            self.half, self.tr, self.arrived, self.me = half, tr, arrived, me
            self.right, self.left = right, left
            opposite = plus(me, 2)
            self.t0 = send(half(opposite, 0), tr(0), right)
            self.t1 = send(half(opposite, 1), tr(1), left)
            self.r1 = send(half(plus(me, 1), 1), arrived(0, 1), right)
            self.l0 = send(half(plus(me, 3), 0), arrived(1, 0), left)

        def forward(self):
            self.t0.wait_recv()
            term = self.half(plus(self.me, 1), 0)
            term[...] = (term[...].astype(F32) + self.tr(0)[...].astype(F32)).astype(BF16)
            self.r0 = send(term, self.arrived(0, 0), self.right)
            self.t1.wait_recv()
            term = self.half(plus(self.me, 3), 1)
            term[...] = (term[...].astype(F32) + self.tr(1)[...].astype(F32)).astype(BF16)
            self.l1 = send(term, self.arrived(1, 1), self.left)

        def finish(self, h):
            (self.r0 if h == 0 else self.r1).wait_recv()
            (self.l0 if h == 0 else self.l1).wait_recv()
            return (
                self.half(self.me, h)[...].astype(F32)
                + self.arrived(0, h)[...].astype(F32)
                + self.arrived(1, h)[...].astype(F32)
            )

    def cot_half(k):
        return cot.at[:, pl.ds(pl.multiple_of(k * 256, 256), 256)]

    cot_wait = transposed(cot_half(c), cot_half(1 - c), ct.at[zh, x, c])

    kv = tensor // 2
    kv_cols = pl.ds(pl.multiple_of(kv * HD, HD), HD)
    key_rows, value_rows = keys[:, kv_cols], values[:, kv_cols]
    starts = jnp.broadcast_to(starts_ref[...] - dp * 128, (128, 128)).T
    row = lax.broadcasted_iota(jnp.int32, (128, 128), 0)
    col = lax.broadcasted_iota(jnp.int32, (128, 128), 1)
    allowed = (col >= starts) & (col <= row)
    for head in range(2):
        scores = lax.dot_general(
            queries[:, head * HD : (head + 1) * HD],
            key_rows,
            (((1,), (1,)), ((), ())),
            preferred_element_type=F32,
        ) / math.sqrt(HD)
        scores = jnp.where(allowed, scores, -1e30)
        top = jnp.max(scores, axis=-1, keepdims=True)
        weights = jnp.where(allowed, jnp.exp(scores - top), 0.0)
        probs = (weights / jnp.sum(weights, axis=-1, keepdims=True)).astype(BF16)
        ho[zh, x, c, :, head * HD : (head + 1) * HD] = jnp.dot(
            probs, value_rows, preferred_element_type=F32
        ).astype(BF16)

    def rows64(h):
        return pl.ds(h * 64, 64)

    def ho_x(g):
        return Gather(
            lambda o: ho.at[g, o, c],
            lambda o, h: ho.at[g, o, c, rows64(h)],
            x,
            x_dev[1],
            x_dev[3],
        )

    def ct_y(g):
        return Gather(
            lambda o: ct.at[g, o], lambda o, h: ct.at[g, o, h], y, y_dev[1], y_dev[3]
        )

    def ho_core(g):
        return send(ho.at[g, :, c], ho.at[g, :, c], sibling)

    ho_z = Gather(
        lambda o: ho.at[o, x, c],
        lambda o, h: ho.at[o, x, c, rows64(h)],
        zh,
        zh_dev[1],
        zh_dev[3],
    )
    groups = [zh, plus(zh, 3), plus(zh, 1), plus(zh, 2)]
    hx = [ho_x(groups[0])]

    cot_wait()
    ct_zl = [send(ct.at[zl, y], ct.at[zl, y], zl_dev[k]) for k in (1, 2, 3)]
    cgroups = [zl, plus(zl, 3), plus(zl, 2), plus(zl, 1)]
    cy = [ct_y(cgroups[0])]

    hx[0].forward()
    ho_z.forward()
    hx.append(ho_x(groups[1]))
    hx.append(ho_x(groups[2]))
    hx[0].finish()
    hc = [ho_core(groups[0])]
    for k in range(3):
        ct_zl[k].wait_recv()
        cy.append(ct_y(cgroups[k + 1]))
    cy[0].forward()

    def project(g):
        def tile(i, carry):
            rows = ho[g, i].reshape(256, 256)
            pp[g, i] = (
                jnp.dot(rows, weight[...], preferred_element_type=F32)
                .astype(BF16)
                .reshape(2, 128, 256)
            )
            return carry

        lax.fori_loop(0, 4, tile, 0)
        return Reduce(
            lambda o, h: pp.at[g, o, h],
            lambda h: p_tr.at[g, h],
            lambda side, h: p_in.at[g, side, h],
            y,
            y_dev[1],
            y_dev[3],
        )

    hc[0].wait_recv()
    py = [project(groups[0])]
    hx[1].forward()
    hx[2].forward()
    ho_z.finish()
    hx.append(ho_x(groups[3]))
    for k in (1, 2):
        hx[k].finish()
        hc.append(ho_core(groups[k]))
    for k in (1, 2, 3):
        cy[k].forward()
    py[0].forward()
    for k in (1, 2):
        hc[k].wait_recv()
        py.append(project(groups[k]))
    hx[3].forward()
    hx[3].finish()
    hc.append(ho_core(groups[3]))
    hc[3].wait_recv()
    py.append(project(groups[3]))

    def heads_grad(g):
        def tile(i, carry):
            rows = ct[g, i].reshape(256, 256)
            gp[g, i] = (
                lax.dot_general(
                    rows, weight[...], (((1,), (1,)), ((), ())), preferred_element_type=F32
                )
                .astype(BF16)
                .reshape(2, 128, 256)
            )
            return carry

        lax.fori_loop(0, 4, tile, 0)
        return send(gp.at[g, :, 1 - c], g_in.at[g], sibling)

    def heads_x(g, from_core):
        from_core.wait_recv()

        def tile(i, carry):
            gs[g, i] = (gp[g, i, c].astype(F32) + g_in[g, i].astype(F32)).astype(BF16)
            return carry

        lax.fori_loop(0, 4, tile, 0)
        return Reduce(
            lambda o, h: gs.at[g, o, rows64(h)],
            lambda h: gx_tr.at[g, h],
            lambda side, h: gx_in.at[g, side, rows64(h)],
            x,
            x_dev[1],
            x_dev[3],
        )

    gc = []
    for k in range(4):
        cy[k].finish()
        gc.append(heads_grad(cgroups[k]))
        if k >= 1:
            py[k].forward()
    gx = [heads_x(cgroups[k], gc[k]) for k in range(4)]

    for k in range(4):
        for h in range(2):
            s_y[groups[k], h] = py[k].finish(h).astype(BF16)
    pz = [send(s_y.at[plus(zl, k)], z_in.at[k - 1], zl_dev[k]) for k in (1, 2, 3)]

    for k in range(4):
        gx[k].forward()
    for k in range(4):
        for h in range(2):
            gh[cgroups[k], rows64(h)] = gx[k].finish(h).astype(BF16)
    gz = Reduce(
        lambda o, h: gh.at[o, rows64(h)],
        lambda h: gz_tr.at[h],
        lambda side, h: gz_in.at[side, rows64(h)],
        zh,
        zh_dev[1],
        zh_dev[3],
    )

    for k in range(3):
        pz[k].wait_recv()
    for h in range(2):
        q_sum[h] = (
            s_y[zl, h].astype(F32)
            + z_in[0, h].astype(F32)
            + z_in[1, h].astype(F32)
            + z_in[2, h].astype(F32)
        ).astype(BF16)
    p_wait = transposed(q_sum.at[c], q_sum.at[1 - c], t_in.at[c])

    acc[...] = jnp.zeros_like(acc)

    def weight_tile(i, carry):
        a, b = i // 4, i % 4
        acc[...] += lax.dot_general(
            ho[a, b].reshape(256, 256),
            ct[a, b].reshape(256, 256),
            (((0,), (0,)), ((), ())),
            preferred_element_type=F32,
        )
        return carry

    lax.fori_loop(0, 16, weight_tile, 0)
    grad_weight[...] = acc[...].astype(BF16)

    gz.forward()

    p_wait()
    squares = jnp.zeros((128, 1), F32)
    for k in range(2):
        cols = slice(k * 256, (k + 1) * 256)
        part = residual[:, cols].astype(F32) + t_in[k].astype(F32)
        stream[:, cols] = part
        mixed[:, cols] = part.astype(BF16)
        squares = squares + jnp.sum(part * part, axis=1, keepdims=True)
    sq[0] = jnp.broadcast_to(squares, (128, 128)).T[:8]
    nz = [send(sq.at[0], sq.at[k], zl_dev[k]) for k in (1, 2, 3)]
    for k in range(3):
        nz[k].wait_recv()
    sq[4] = sq[0] + sq[1] + sq[2] + sq[3]
    ny = [send(sq.at[4], sq.at[4 + k], y_dev[k]) for k in (1, 2, 3)]

    for h in range(2):
        grad_heads[h * 64 : (h + 1) * 64, :] = gz.finish(h).astype(BF16)

    for k in range(3):
        ny[k].wait_recv()
    total = sq[4] + sq[5] + sq[6] + sq[7]
    mean_square = jnp.broadcast_to(total[:1], (128, 128)).T[:, :1] / D_MODEL
    factor = lax.rsqrt(mean_square + EPS)
    normed[...] = (stream[...] * factor * gain[...].astype(F32)).astype(BF16)

    for made in sent:
        made.wait_send()


def body(queries, keys, values, doc_start, out_weight, residual, gain, cotangent):
    vmem = pl.BlockSpec(memory_space=pltpu.VMEM)

    def buf(*shape):
        return pltpu.VMEM(shape, BF16)

    return pl.pallas_call(
        kernel,
        out_shape=(
            jax.ShapeDtypeStruct((128, 512), BF16),
            jax.ShapeDtypeStruct((128, 512), BF16),
            jax.ShapeDtypeStruct((256, 256), BF16),
            jax.ShapeDtypeStruct((128, 256), BF16),
        ),
        in_specs=[vmem] * 8,
        out_specs=(vmem,) * 4,
        scratch_shapes=[
            buf(4, 4, 2, 128, 256),
            buf(4, 4, 2, 128, 256),
            buf(4, 4, 2, 128, 256),
            buf(4, 2, 128, 256),
            buf(4, 2, 2, 128, 256),
            buf(4, 2, 128, 256),
            buf(3, 2, 128, 256),
            buf(2, 128, 256),
            buf(2, 128, 256),
            buf(4, 4, 2, 128, 256),
            buf(4, 4, 128, 256),
            buf(4, 4, 128, 256),
            buf(4, 2, 64, 256),
            buf(4, 2, 128, 256),
            buf(4, 128, 256),
            buf(2, 64, 256),
            buf(2, 128, 256),
            pltpu.VMEM((128, 512), F32),
            pltpu.VMEM((8, 8, 128), F32),
            pltpu.VMEM((256, 256), F32),
            pltpu.SemaphoreType.DMA((N_COPIES,)),
            pltpu.SemaphoreType.DMA((N_COPIES,)),
        ],
        compiler_params=pltpu.CompilerParams(
            collective_id=0, has_side_effects=True, vmem_limit_bytes=32 * 2**20
        ),
    )(
        queries,
        keys,
        values,
        doc_start.reshape(1, 128),
        out_weight,
        residual,
        gain.reshape(1, 512),
        cotangent,
    )


def solution(mesh):
    placed = (
        P("dp", "tensor"),
        P("dp", None),
        P("dp", None),
        P("dp"),
        P("tensor", "dp"),
        P("dp", "tensor"),
        P("tensor"),
        P("dp", "tensor"),
    )
    return jax.shard_map(
        body,
        mesh=mesh,
        in_specs=placed,
        out_specs=(P("dp", "tensor"), P("dp", "tensor"), P("tensor", "dp"), P("dp", "tensor")),
        check_vma=False,
    )
```

```python
import functools
import math

import jax
import jax.numpy as jnp
from jax import lax
from jax.experimental import pallas as pl
from jax.experimental.pallas import tpu as pltpu
from jax.sharding import PartitionSpec as P

HD = 128
EPS = 1e-05
D_MODEL = 8192
MESH = pl.DeviceIdType.MESH
BF16 = jnp.bfloat16
F32 = jnp.float32
N_COPIES = 176
N_LOADS = 8


def kernel(
    queries_hbm,
    keys_hbm,
    values_hbm,
    starts_hbm,
    weight_hbm,
    residual_hbm,
    gain_hbm,
    cot_hbm,
    mixed,
    normed,
    grad_weight,
    grad_heads,
    mine,
    ho,
    ct,
    wt,
    s_y,
    z_in,
    q_sum,
    t_in,
    gw,
    gw_tr,
    gw_in,
    gp,
    g_in,
    gs,
    gx_tr,
    gx_in,
    gh,
    gz_tr,
    gz_in,
    g_sum,
    g_land,
    stream,
    sq,
    queries,
    keys,
    values,
    starts_ref,
    residual,
    gain,
    cot,
    ssem,
    rsem,
    lsem,
):
    dp, tensor = lax.axis_index("dp"), lax.axis_index("tensor")
    zh, x, c = dp // 8, (dp // 2) % 4, dp % 2
    zl, y = tensor // 4, tensor % 4

    def dev(zh_, x_, c_, zl_, y_):
        return ((zh_ * 4 + x_) * 2 + c_, zl_ * 4 + y_)

    def plus(a, k):
        return (a + k) % 4

    y_dev = {k: dev(zh, x, c, zl, plus(y, k)) for k in (1, 3)}
    zl_dev = {k: dev(zh, x, c, plus(zl, k), y) for k in (1, 2, 3)}
    row_dev = {k: (dp, (tensor + k) % 16) for k in range(1, 16)}
    x_dev = {k: dev(zh, plus(x, k), c, zl, y) for k in (1, 3)}
    zh_dev = {k: dev(plus(zh, k), x, c, zl, y) for k in (1, 3)}
    sibling = dev(zh, x, 1 - c, zl, y)
    t_same, t_other = dev(zl, y, c, zh, x), dev(zl, y, 1 - c, zh, x)
    off_diagonal = (zh != zl) | (x != y)
    on_diagonal = (zh == zl) & (x == y)
    xy_dev = dev(zh, y, c, zl, x)

    kv = tensor // 2
    kv_cols = pl.ds(pl.multiple_of(kv * HD, HD), HD)
    loads = [
        pltpu.make_async_copy(src, dst, lsem.at[index])
        for index, (src, dst) in enumerate(
            (
                (cot_hbm, cot),
                (queries_hbm, queries),
                (keys_hbm.at[:, kv_cols], keys),
                (values_hbm.at[:, kv_cols], values),
                (starts_hbm, starts_ref),
                (weight_hbm, wt.at[y]),
                (residual_hbm, residual),
                (gain_hbm, gain),
            )
        )
    ]
    for load in loads:
        load.start()

    barrier = pltpu.get_barrier_semaphore()
    partners = [*row_dev.values(), *x_dev.values(), *zh_dev.values(), sibling]
    for partner in partners:
        pl.semaphore_signal(barrier, inc=1, device_id=partner, device_id_type=MESH)

    @pl.when(off_diagonal)
    def _():
        for partner in (t_same, t_other):
            pl.semaphore_signal(barrier, inc=1, device_id=partner, device_id_type=MESH)

    @pl.when(x != y)
    def _():
        pl.semaphore_signal(barrier, inc=1, device_id=xy_dev, device_id_type=MESH)
        pl.semaphore_wait(barrier, len(partners) + 3)

    @pl.when((x == y) & (zh != zl))
    def _():
        pl.semaphore_wait(barrier, len(partners) + 2)

    @pl.when(on_diagonal)
    def _():
        pl.semaphore_wait(barrier, len(partners))

    for load in loads:
        load.wait()

    sent = []
    used = [0]

    def copy(src, dst, device):
        index = used[0]
        used[0] += 1
        return pltpu.make_async_remote_copy(
            src_ref=src,
            dst_ref=dst,
            send_sem=ssem.at[index],
            recv_sem=rsem.at[index],
            device_id=device,
            device_id_type=MESH,
        )

    def send(src, dst, device):
        made = copy(src, dst, device)
        made.start()
        sent.append(made)
        return made

    def transposed(own_src, other_src, dst):
        other = send(other_src, dst, t_other)
        same = copy(own_src, dst, t_same)

        @pl.when(off_diagonal)
        def _():
            same.start()

        @pl.when(on_diagonal)
        def _():
            dst[...] = own_src[...]

        def wait():
            other.wait_recv()

            @pl.when(off_diagonal)
            def _():
                same.wait()

        return wait

    def swapped(src, dst):
        made = copy(src, dst, xy_dev)

        @pl.when(x != y)
        def _():
            made.start()

        @pl.when(x == y)
        def _():
            dst[...] = src[...]

        def wait():
            @pl.when(x != y)
            def _():
                made.wait()

        return wait

    class Gather:
        def __init__(self, half, me, right, left):
            self.half, self.me, self.right, self.left = half, me, right, left
            self.right0 = send(half(me, 0), half(me, 0), right)
            self.left1 = send(half(me, 1), half(me, 1), left)
            self.right1 = send(half(me, 1), half(me, 1), right)
            self.left0 = send(half(me, 0), half(me, 0), left)

        def forward(self):
            self.right0.wait_recv()
            half = self.half(plus(self.me, 3), 0)
            self.on_right = send(half, half, self.right)
            self.left1.wait_recv()
            half = self.half(plus(self.me, 1), 1)
            self.on_left = send(half, half, self.left)

        def neighbours(self):
            self.right1.wait_recv()
            self.left0.wait_recv()

        def finish(self):
            self.on_right.wait_recv()
            self.on_left.wait_recv()

    class Reduce:
        def __init__(self, half, tr, arrived, me, right, left):
            self.half, self.tr, self.arrived, self.me = half, tr, arrived, me
            self.right, self.left = right, left
            opposite = plus(me, 2)
            self.t0 = send(half(opposite, 0), tr(0), right)
            self.t1 = send(half(opposite, 1), tr(1), left)
            self.r1 = send(half(plus(me, 1), 1), arrived(0, 1), right)
            self.l0 = send(half(plus(me, 3), 0), arrived(1, 0), left)

        def forward(self):
            self.t0.wait_recv()
            term = self.half(plus(self.me, 1), 0)
            term[...] = (term[...].astype(F32) + self.tr(0)[...].astype(F32)).astype(BF16)
            self.r0 = send(term, self.arrived(0, 0), self.right)
            self.t1.wait_recv()
            term = self.half(plus(self.me, 3), 1)
            term[...] = (term[...].astype(F32) + self.tr(1)[...].astype(F32)).astype(BF16)
            self.l1 = send(term, self.arrived(1, 1), self.left)

        def finish(self, h):
            (self.r0 if h == 0 else self.r1).wait_recv()
            (self.l0 if h == 0 else self.l1).wait_recv()
            return (
                self.half(self.me, h)[...].astype(F32)
                + self.arrived(0, h)[...].astype(F32)
                + self.arrived(1, h)[...].astype(F32)
            )

    def cot_half(k):
        return cot.at[:, pl.ds(pl.multiple_of(k * 256, 256), 256)]

    cot_wait = transposed(cot_half(c), cot_half(1 - c), ct.at[zh, c])
    w_y = Gather(lambda o, h: wt.at[o, pl.ds(h * 128, 128)], y, y_dev[1], y_dev[3])

    key_rows, value_rows = keys[...], values[...]
    starts = jnp.broadcast_to(starts_ref[...] - dp * 128, (128, 128)).T
    row = lax.broadcasted_iota(jnp.int32, (128, 128), 0)
    col = lax.broadcasted_iota(jnp.int32, (128, 128), 1)
    allowed = (col >= starts) & (col <= row)
    for head in range(2):
        scores = lax.dot_general(
            queries[:, head * HD : (head + 1) * HD],
            key_rows,
            (((1,), (1,)), ((), ())),
            preferred_element_type=F32,
        ) / math.sqrt(HD)
        scores = jnp.where(allowed, scores, -1e30)
        top = jnp.max(scores, axis=-1, keepdims=True)
        weights = jnp.where(allowed, jnp.exp(scores - top), 0.0)
        probs = (weights / jnp.sum(weights, axis=-1, keepdims=True)).astype(BF16)
        mine[:, head * HD : (head + 1) * HD] = jnp.dot(
            probs, value_rows, preferred_element_type=F32
        ).astype(BF16)

    def rows64(h):
        return pl.ds(h * 64, 64)

    def ho_x(g):
        return Gather(lambda o, h: ho.at[g, o, c, rows64(h)], x, x_dev[1], x_dev[3])

    def ho_core(g):
        return send(ho.at[g, :, c], ho.at[g, :, c], sibling)

    z_base = used[0]
    used[0] += 4

    def z_copy(k, src):
        return pltpu.make_async_remote_copy(
            src_ref=src,
            dst_ref=z_in.at[k],
            send_sem=ssem.at[z_base + k],
            recv_sem=rsem.at[z_base + k],
            device_id=dev(zh, x, c, plus(zl, k), y),
            device_id_type=MESH,
        )

    def project(g):
        part = jnp.dot(ho[g, 0].reshape(256, 256), wt[0], preferred_element_type=F32)
        for i in range(1, 4):
            part = part + jnp.dot(
                ho[g, i].reshape(256, 256), wt[i], preferred_element_type=F32
            )
        s_y[g] = part.astype(BF16).reshape(2, 128, 256)
        k = plus(g, 4 - zl)

        @pl.when(k != 0)
        def _():
            z_copy(k, s_y.at[g]).start()

    def heads_grad(g):
        def tile(i, carry):
            gp[g, i] = (
                lax.dot_general(
                    ct[g].reshape(256, 256),
                    wt[i],
                    (((1,), (1,)), ((), ())),
                    preferred_element_type=F32,
                )
                .astype(BF16)
                .reshape(2, 128, 256)
            )
            return carry

        lax.fori_loop(0, 4, tile, 0)
        return send(gp.at[g, :, 1 - c], g_in.at[g], sibling)

    def heads_x(g, from_core):
        from_core.wait_recv()

        def tile(i, carry):
            gs[g, i] = (gp[g, i, c].astype(F32) + g_in[g, i].astype(F32)).astype(BF16)
            return carry

        lax.fori_loop(0, 4, tile, 0)
        return Reduce(
            lambda o, h: gs.at[g, o, rows64(h)],
            lambda h: gx_tr.at[g, h],
            lambda side, h: gx_in.at[g, side, rows64(h)],
            x,
            x_dev[1],
            x_dev[3],
        )

    mine_wait = swapped(mine, ho.at[zh, y, c])
    w_y.forward()
    mine_wait()
    ho_z = Gather(lambda o, h: ho.at[o, x, c, rows64(h)], zh, zh_dev[1], zh_dev[3])
    groups = [zh, plus(zh, 3), plus(zh, 1), plus(zh, 2)]
    cgroups = [zl, plus(zl, 3), plus(zl, 2), plus(zl, 1)]
    hx = [ho_x(groups[0])]
    cot_wait()
    ct_zl = [send(ct.at[zl], ct.at[zl], zl_dev[k]) for k in (1, 2, 3)]
    hx[0].forward()
    w_y.neighbours()
    w_y.finish()
    gc = [heads_grad(cgroups[0])]
    hx[0].neighbours()
    hx[0].finish()
    hc = [ho_core(groups[0])]
    ho_z.forward()
    ho_z.neighbours()
    hx.append(ho_x(groups[1]))
    hx.append(ho_x(groups[2]))
    hc[0].wait_recv()
    project(groups[0])
    gx = [heads_x(cgroups[0], gc[0])]
    hx[1].forward()
    hx[2].forward()
    ho_z.finish()
    hx.append(ho_x(groups[3]))
    for k in (1, 2):
        hx[k].neighbours()
        hx[k].finish()
        hc.append(ho_core(groups[k]))
    hx[3].forward()
    for k in (1, 2):
        hc[k].wait_recv()
        project(groups[k])
    hx[3].neighbours()
    hx[3].finish()
    hc.append(ho_core(groups[3]))
    hc[3].wait_recv()
    project(groups[3])
    for k in (1, 2, 3):
        ct_zl[k - 1].wait_recv()
        gc.append(heads_grad(cgroups[k]))
    for k in (1, 2, 3):
        gx.append(heads_x(cgroups[k], gc[k]))
    for k in range(4):
        gx[k].forward()

    def weight_tile(i, carry):
        part = jnp.zeros((256, 256), F32)
        for g in range(4):
            part = part + lax.dot_general(
                ho[g, i].reshape(256, 256),
                ct[g].reshape(256, 256),
                (((0,), (0,)), ((), ())),
                preferred_element_type=F32,
            )
        gw[i] = part.astype(BF16)
        return carry

    lax.fori_loop(0, 4, weight_tile, 0)
    gw_y = Reduce(
        lambda o, h: gw.at[o, pl.ds(h * 128, 128)],
        lambda h: gw_tr.at[h],
        lambda side, h: gw_in.at[side, pl.ds(h * 128, 128)],
        y,
        y_dev[1],
        y_dev[3],
    )

    for k in range(4):
        for h in range(2):
            gh[cgroups[k], rows64(h)] = gx[k].finish(h).astype(BF16)
    gz = Reduce(
        lambda o, h: gh.at[o, rows64(h)],
        lambda h: gz_tr.at[h],
        lambda side, h: gz_in.at[side, rows64(h)],
        zh,
        zh_dev[1],
        zh_dev[3],
    )

    for k in (1, 2, 3):
        z_copy(k, s_y.at[0]).wait_recv()
    for h in range(2):
        q_sum[h] = (
            s_y[zl, h].astype(F32)
            + z_in[1, h].astype(F32)
            + z_in[2, h].astype(F32)
            + z_in[3, h].astype(F32)
        ).astype(BF16)
    p_wait = transposed(q_sum.at[c], q_sum.at[1 - c], t_in.at[c])

    gw_y.forward()
    gz.forward()
    for h in range(2):
        grad_weight[h * 128 : (h + 1) * 128, :] = gw_y.finish(h).astype(BF16)

    p_wait()
    squares = jnp.zeros((128, 1), F32)
    for k in range(2):
        cols = slice(k * 256, (k + 1) * 256)
        part = residual[:, cols].astype(F32) + t_in[k].astype(F32)
        stream[:, cols] = part
        mixed[:, cols] = part.astype(BF16)
        squares = squares + jnp.sum(part * part, axis=1, keepdims=True)
    sq[0] = jnp.broadcast_to(squares, (128, 128)).T[:8]
    norms = [send(sq.at[0], sq.at[k], row_dev[k]) for k in range(1, 16)]

    for h in range(2):
        g_sum[h * 64 : (h + 1) * 64, :] = gz.finish(h).astype(BF16)
    g_wait = swapped(g_sum, g_land)

    for made in norms:
        made.wait_recv()
    total = jnp.sum(sq[...], axis=0)
    mean_square = jnp.broadcast_to(total[:1], (128, 128)).T[:, :1] / D_MODEL
    factor = lax.rsqrt(mean_square + EPS)
    normed[...] = (stream[...] * factor * gain[...].astype(F32)).astype(BF16)

    g_wait()
    grad_heads[...] = g_land[...]

    for made in sent:
        made.wait_send()
    for k in (1, 2, 3):
        z_copy(k, s_y.at[0]).wait_send()


def body(queries, keys, values, doc_start, out_weight, residual, gain, cotangent):
    vmem = pl.BlockSpec(memory_space=pltpu.VMEM)

    def buf(*shape):
        return pltpu.VMEM(shape, BF16)

    return pl.pallas_call(
        kernel,
        out_shape=(
            jax.ShapeDtypeStruct((128, 512), BF16),
            jax.ShapeDtypeStruct((128, 512), BF16),
            jax.ShapeDtypeStruct((256, 256), BF16),
            jax.ShapeDtypeStruct((128, 256), BF16),
        ),
        in_specs=[pl.BlockSpec(memory_space=pltpu.HBM)] * 8,
        out_specs=(vmem,) * 4,
        scratch_shapes=[
            buf(128, 256),
            buf(4, 4, 2, 128, 256),
            buf(4, 2, 128, 256),
            buf(4, 256, 256),
            buf(4, 2, 128, 256),
            buf(4, 2, 128, 256),
            buf(2, 128, 256),
            buf(2, 128, 256),
            buf(4, 256, 256),
            buf(2, 128, 256),
            buf(2, 256, 256),
            buf(4, 4, 2, 128, 256),
            buf(4, 4, 128, 256),
            buf(4, 4, 128, 256),
            buf(4, 2, 64, 256),
            buf(4, 2, 128, 256),
            buf(4, 128, 256),
            buf(2, 64, 256),
            buf(2, 128, 256),
            buf(128, 256),
            buf(128, 256),
            pltpu.VMEM((128, 512), F32),
            pltpu.VMEM((16, 8, 128), F32),
            buf(128, 256),
            buf(128, 128),
            buf(128, 128),
            pltpu.VMEM((1, 128), jnp.int32),
            buf(128, 512),
            buf(1, 512),
            buf(128, 512),
            pltpu.SemaphoreType.DMA((N_COPIES,)),
            pltpu.SemaphoreType.DMA((N_COPIES,)),
            pltpu.SemaphoreType.DMA((N_LOADS,)),
        ],
        compiler_params=pltpu.CompilerParams(
            collective_id=0, has_side_effects=True, vmem_limit_bytes=32 * 2**20
        ),
    )(
        queries,
        keys,
        values,
        doc_start.reshape(1, 128),
        out_weight,
        residual,
        gain.reshape(1, 512),
        cotangent,
    )


def solution(mesh):
    placed = (
        P("dp", "tensor"),
        P("dp", None),
        P("dp", None),
        P("dp"),
        P("tensor", "dp"),
        P("dp", "tensor"),
        P("tensor"),
        P("dp", "tensor"),
    )
    return jax.shard_map(
        body,
        mesh=mesh,
        in_specs=placed,
        out_specs=(P("dp", "tensor"), P("dp", "tensor"), P("tensor", "dp"), P("dp", "tensor")),
        check_vma=False,
    )
```

```python
import functools
import math

import jax
import jax.numpy as jnp
from jax import lax
from jax.experimental import pallas as pl
from jax.experimental.pallas import tpu as pltpu
from jax.sharding import PartitionSpec as P

HD = 128
EPS = 1e-05
D_MODEL = 8192
MESH = pl.DeviceIdType.MESH
BF16 = jnp.bfloat16
F32 = jnp.float32
N_COPIES = 176
N_LOADS = 8


def kernel(
    queries_hbm,
    keys_hbm,
    values_hbm,
    starts_hbm,
    weight_hbm,
    residual_hbm,
    gain_hbm,
    cot_hbm,
    mixed,
    normed,
    grad_weight,
    grad_heads,
    mine,
    ho,
    ct,
    wt,
    s_y,
    z_in,
    q_sum,
    t_in,
    gw,
    gw_tr,
    gw_in,
    gp,
    g_in,
    gs,
    gx_tr,
    gx_in,
    gh,
    gz_tr,
    gz_in,
    g_own,
    stream,
    sq,
    queries,
    keys,
    values,
    starts_ref,
    residual,
    gain,
    cot,
    ssem,
    rsem,
    lsem,
):
    dp, tensor = lax.axis_index("dp"), lax.axis_index("tensor")
    zh, x, c = dp // 8, (dp // 2) % 4, dp % 2
    zl, y = tensor // 4, tensor % 4

    def dev(zh_, x_, c_, zl_, y_):
        return ((zh_ * 4 + x_) * 2 + c_, zl_ * 4 + y_)

    def plus(a, k):
        return (a + k) % 4

    y_dev = {k: dev(zh, x, c, zl, plus(y, k)) for k in (1, 3)}
    zl_dev = {k: dev(zh, x, c, plus(zl, k), y) for k in (1, 2, 3)}
    row_dev = {k: (dp, (tensor + k) % 16) for k in range(1, 16)}
    x_dev = {k: dev(zh, plus(x, k), c, zl, y) for k in (1, 3)}
    zh_dev = {k: dev(plus(zh, k), x, c, zl, y) for k in (1, 3)}
    sibling = dev(zh, x, 1 - c, zl, y)
    t_same, t_other = dev(zl, y, c, zh, x), dev(zl, y, 1 - c, zh, x)
    off_diagonal = (zh != zl) | (x != y)
    on_diagonal = (zh == zl) & (x == y)
    xy_dev = dev(zh, y, c, zl, x)
    xy_zh_dev = {k: dev(plus(zh, k), y, c, zl, x) for k in (1, 3)}

    kv = tensor // 2
    kv_cols = pl.ds(pl.multiple_of(kv * HD, HD), HD)
    loads = [
        pltpu.make_async_copy(src, dst, lsem.at[index])
        for index, (src, dst) in enumerate(
            (
                (cot_hbm, cot),
                (queries_hbm, queries),
                (keys_hbm.at[:, kv_cols], keys),
                (values_hbm.at[:, kv_cols], values),
                (starts_hbm, starts_ref),
                (weight_hbm, wt.at[y]),
                (residual_hbm, residual),
                (gain_hbm, gain),
            )
        )
    ]
    for load in loads:
        load.start()

    barrier = pltpu.get_barrier_semaphore()
    partners = [
        *row_dev.values(),
        *x_dev.values(),
        *zh_dev.values(),
        *xy_zh_dev.values(),
        sibling,
    ]
    for partner in partners:
        pl.semaphore_signal(barrier, inc=1, device_id=partner, device_id_type=MESH)

    @pl.when(off_diagonal)
    def _():
        for partner in (t_same, t_other):
            pl.semaphore_signal(barrier, inc=1, device_id=partner, device_id_type=MESH)

    @pl.when(x != y)
    def _():
        pl.semaphore_signal(barrier, inc=1, device_id=xy_dev, device_id_type=MESH)
        pl.semaphore_wait(barrier, len(partners) + 3)

    @pl.when((x == y) & (zh != zl))
    def _():
        pl.semaphore_wait(barrier, len(partners) + 2)

    @pl.when(on_diagonal)
    def _():
        pl.semaphore_wait(barrier, len(partners))

    for load in loads:
        load.wait()

    sent = []
    used = [0]

    def copy(src, dst, device):
        index = used[0]
        used[0] += 1
        return pltpu.make_async_remote_copy(
            src_ref=src,
            dst_ref=dst,
            send_sem=ssem.at[index],
            recv_sem=rsem.at[index],
            device_id=device,
            device_id_type=MESH,
        )

    def send(src, dst, device):
        made = copy(src, dst, device)
        made.start()
        sent.append(made)
        return made

    def transposed(own_src, other_src, dst):
        other = send(other_src, dst, t_other)
        same = copy(own_src, dst, t_same)

        @pl.when(off_diagonal)
        def _():
            same.start()

        @pl.when(on_diagonal)
        def _():
            dst[...] = own_src[...]

        def wait():
            other.wait_recv()

            @pl.when(off_diagonal)
            def _():
                same.wait()

        return wait

    def swapped(src, dst):
        made = copy(src, dst, xy_dev)

        @pl.when(x != y)
        def _():
            made.start()

        @pl.when(x == y)
        def _():
            dst[...] = src[...]

        def wait():
            @pl.when(x != y)
            def _():
                made.wait()

        return wait

    class Gather:
        def __init__(self, half, me, right, left, first=None):
            self.half, self.me, self.right, self.left = half, me, right, left
            src = dst = functools.partial(half, me)
            if first is not None:
                src, dst, right, left = first
            self.right0 = send(src(0), dst(0), right)
            self.left1 = send(src(1), dst(1), left)
            self.right1 = send(src(1), dst(1), right)
            self.left0 = send(src(0), dst(0), left)

        def forward(self):
            self.right0.wait_recv()
            half = self.half(plus(self.me, 3), 0)
            self.on_right = send(half, half, self.right)
            self.left1.wait_recv()
            half = self.half(plus(self.me, 1), 1)
            self.on_left = send(half, half, self.left)

        def neighbours(self):
            self.right1.wait_recv()
            self.left0.wait_recv()

        def finish(self):
            self.on_right.wait_recv()
            self.on_left.wait_recv()

    class Reduce:
        def __init__(self, half, tr, arrived, me, right, left, last=None):
            self.half, self.tr, self.arrived, self.me = half, tr, arrived, me
            last_right, last_left = (right, left) if last is None else last
            self.right, self.left = last_right, last_left
            opposite = plus(me, 2)
            self.t0 = send(half(opposite, 0), tr(0), right)
            self.t1 = send(half(opposite, 1), tr(1), left)
            self.r1 = send(half(plus(me, 1), 1), arrived(0, 1), last_right)
            self.l0 = send(half(plus(me, 3), 0), arrived(1, 0), last_left)

        def forward(self):
            self.t0.wait_recv()
            term = self.half(plus(self.me, 1), 0)
            term[...] = (term[...].astype(F32) + self.tr(0)[...].astype(F32)).astype(BF16)
            self.r0 = send(term, self.arrived(0, 0), self.right)
            self.t1.wait_recv()
            term = self.half(plus(self.me, 3), 1)
            term[...] = (term[...].astype(F32) + self.tr(1)[...].astype(F32)).astype(BF16)
            self.l1 = send(term, self.arrived(1, 1), self.left)

        def finish(self, h, own=None):
            own = self.half(self.me, h) if own is None else own
            (self.r0 if h == 0 else self.r1).wait_recv()
            (self.l0 if h == 0 else self.l1).wait_recv()
            return (
                own[...].astype(F32)
                + self.arrived(0, h)[...].astype(F32)
                + self.arrived(1, h)[...].astype(F32)
            )

    def cot_half(k):
        return cot.at[:, pl.ds(pl.multiple_of(k * 256, 256), 256)]

    cot_wait = transposed(cot_half(c), cot_half(1 - c), ct.at[zh, c])
    w_y = Gather(lambda o, h: wt.at[o, pl.ds(h * 128, 128)], y, y_dev[1], y_dev[3])

    key_rows, value_rows = keys[...], values[...]
    starts = jnp.broadcast_to(starts_ref[...] - dp * 128, (128, 128)).T
    row = lax.broadcasted_iota(jnp.int32, (128, 128), 0)
    col = lax.broadcasted_iota(jnp.int32, (128, 128), 1)
    allowed = (col >= starts) & (col <= row)
    for head in range(2):
        scores = lax.dot_general(
            queries[:, head * HD : (head + 1) * HD],
            key_rows,
            (((1,), (1,)), ((), ())),
            preferred_element_type=F32,
        ) / math.sqrt(HD)
        scores = jnp.where(allowed, scores, -1e30)
        top = jnp.max(scores, axis=-1, keepdims=True)
        weights = jnp.where(allowed, jnp.exp(scores - top), 0.0)
        probs = (weights / jnp.sum(weights, axis=-1, keepdims=True)).astype(BF16)
        mine[:, head * HD : (head + 1) * HD] = jnp.dot(
            probs, value_rows, preferred_element_type=F32
        ).astype(BF16)

    def rows64(h):
        return pl.ds(h * 64, 64)

    def ho_x(g):
        return Gather(lambda o, h: ho.at[g, o, c, rows64(h)], x, x_dev[1], x_dev[3])

    def ho_core(g):
        return send(ho.at[g, :, c], ho.at[g, :, c], sibling)

    z_base = used[0]
    used[0] += 4

    def z_copy(k, src):
        return pltpu.make_async_remote_copy(
            src_ref=src,
            dst_ref=z_in.at[k],
            send_sem=ssem.at[z_base + k],
            recv_sem=rsem.at[z_base + k],
            device_id=dev(zh, x, c, plus(zl, k), y),
            device_id_type=MESH,
        )

    def project(g):
        part = jnp.dot(ho[g, 0].reshape(256, 256), wt[0], preferred_element_type=F32)
        for i in range(1, 4):
            part = part + jnp.dot(
                ho[g, i].reshape(256, 256), wt[i], preferred_element_type=F32
            )
        s_y[g] = part.astype(BF16).reshape(2, 128, 256)
        k = plus(g, 4 - zl)

        @pl.when(k != 0)
        def _():
            z_copy(k, s_y.at[g]).start()

    def heads_grad(g):
        def tile(i, carry):
            gp[g, i] = (
                lax.dot_general(
                    ct[g].reshape(256, 256),
                    wt[i],
                    (((1,), (1,)), ((), ())),
                    preferred_element_type=F32,
                )
                .astype(BF16)
                .reshape(2, 128, 256)
            )
            return carry

        lax.fori_loop(0, 4, tile, 0)
        return send(gp.at[g, :, 1 - c], g_in.at[g], sibling)

    def heads_x(g, from_core):
        from_core.wait_recv()

        def tile(i, carry):
            gs[g, i] = (gp[g, i, c].astype(F32) + g_in[g, i].astype(F32)).astype(BF16)
            return carry

        lax.fori_loop(0, 4, tile, 0)
        return Reduce(
            lambda o, h: gs.at[g, o, rows64(h)],
            lambda h: gx_tr.at[g, h],
            lambda side, h: gx_in.at[g, side, rows64(h)],
            x,
            x_dev[1],
            x_dev[3],
        )

    ho_z = Gather(
        lambda o, h: ho.at[o, x, c, rows64(h)],
        zh,
        zh_dev[1],
        zh_dev[3],
        (
            lambda h: mine.at[rows64(h)],
            lambda h: ho.at[zh, y, c, rows64(h)],
            xy_zh_dev[1],
            xy_zh_dev[3],
        ),
    )
    mine_wait = swapped(mine, ho.at[zh, y, c])
    groups = [zh, plus(zh, 3), plus(zh, 1), plus(zh, 2)]
    cgroups = [zl, plus(zl, 3), plus(zl, 2), plus(zl, 1)]
    w_y.forward()
    mine_wait()
    hx = [ho_x(groups[0])]
    ho_z.forward()
    cot_wait()
    ct_zl = [send(ct.at[zl], ct.at[zl], zl_dev[k]) for k in (1, 2, 3)]
    hx[0].forward()
    w_y.neighbours()
    w_y.finish()
    gc = [heads_grad(cgroups[0])]
    ho_z.neighbours()
    hx.append(ho_x(groups[1]))
    hx.append(ho_x(groups[2]))
    hx[0].neighbours()
    hx[0].finish()
    hc = [ho_core(groups[0])]
    gx = [heads_x(cgroups[0], gc[0])]
    hc[0].wait_recv()
    project(groups[0])
    hx[1].forward()
    hx[2].forward()
    ho_z.finish()
    hx.append(ho_x(groups[3]))
    for k in (1, 2):
        hx[k].neighbours()
        hx[k].finish()
        hc.append(ho_core(groups[k]))
    for k in (1, 2, 3):
        ct_zl[k - 1].wait_recv()
        gc.append(heads_grad(cgroups[k]))
        if k < 3:
            hc[k].wait_recv()
            project(groups[k])
    hx[3].forward()
    for k in (1, 2, 3):
        gx.append(heads_x(cgroups[k], gc[k]))
    gx[0].forward()
    hx[3].neighbours()
    hx[3].finish()
    hc.append(ho_core(groups[3]))
    hc[3].wait_recv()
    project(groups[3])
    for k in (1, 2, 3):
        gx[k].forward()
    for k in range(4):
        for h in range(2):
            gh[cgroups[k], rows64(h)] = gx[k].finish(h).astype(BF16)
    gz = Reduce(
        lambda o, h: gh.at[o, rows64(h)],
        lambda h: gz_tr.at[h],
        lambda side, h: gz_in.at[side, rows64(h)],
        zh,
        zh_dev[1],
        zh_dev[3],
        (xy_zh_dev[1], xy_zh_dev[3]),
    )
    own_wait = swapped(gh.at[zh], g_own)

    for k in (1, 2, 3):
        z_copy(k, s_y.at[0]).wait_recv()
    for h in range(2):
        q_sum[h] = (
            s_y[zl, h].astype(F32)
            + z_in[1, h].astype(F32)
            + z_in[2, h].astype(F32)
            + z_in[3, h].astype(F32)
        ).astype(BF16)
    p_wait = transposed(q_sum.at[c], q_sum.at[1 - c], t_in.at[c])

    def weight_tile(i, carry):
        part = jnp.zeros((256, 256), F32)
        for g in range(4):
            part = part + lax.dot_general(
                ho[g, i].reshape(256, 256),
                ct[g].reshape(256, 256),
                (((0,), (0,)), ((), ())),
                preferred_element_type=F32,
            )
        gw[i] = part.astype(BF16)
        return carry

    lax.fori_loop(0, 4, weight_tile, 0)
    gw_y = Reduce(
        lambda o, h: gw.at[o, pl.ds(h * 128, 128)],
        lambda h: gw_tr.at[h],
        lambda side, h: gw_in.at[side, pl.ds(h * 128, 128)],
        y,
        y_dev[1],
        y_dev[3],
    )
    gz.forward()
    gw_y.forward()

    p_wait()
    squares = jnp.zeros((128, 1), F32)
    for k in range(2):
        cols = slice(k * 256, (k + 1) * 256)
        part = residual[:, cols].astype(F32) + t_in[k].astype(F32)
        stream[:, cols] = part
        mixed[:, cols] = part.astype(BF16)
        squares = squares + jnp.sum(part * part, axis=1, keepdims=True)
    sq[0] = jnp.broadcast_to(squares, (128, 128)).T[:8]
    norms = [send(sq.at[0], sq.at[k], row_dev[k]) for k in range(1, 16)]

    for h in range(2):
        grad_weight[h * 128 : (h + 1) * 128, :] = gw_y.finish(h).astype(BF16)
    own_wait()
    for h in range(2):
        rows = g_own.at[rows64(h)]
        grad_heads[h * 64 : (h + 1) * 64, :] = gz.finish(h, rows).astype(BF16)

    for made in norms:
        made.wait_recv()
    total = jnp.sum(sq[...], axis=0)
    mean_square = jnp.broadcast_to(total[:1], (128, 128)).T[:, :1] / D_MODEL
    factor = lax.rsqrt(mean_square + EPS)
    for k in range(4):
        cols = slice(k * 128, (k + 1) * 128)
        normed[:, cols] = (stream[:, cols] * factor * gain[k : k + 1, :].astype(F32)).astype(BF16)

    for made in sent:
        made.wait_send()
    for k in (1, 2, 3):
        z_copy(k, s_y.at[0]).wait_send()


def body(queries, keys, values, doc_start, out_weight, residual, gain, cotangent):
    vmem = pl.BlockSpec(memory_space=pltpu.VMEM)

    def buf(*shape):
        return pltpu.VMEM(shape, BF16)

    return pl.pallas_call(
        kernel,
        out_shape=(
            jax.ShapeDtypeStruct((128, 512), BF16),
            jax.ShapeDtypeStruct((128, 512), BF16),
            jax.ShapeDtypeStruct((256, 256), BF16),
            jax.ShapeDtypeStruct((128, 256), BF16),
        ),
        in_specs=[pl.BlockSpec(memory_space=pltpu.HBM)] * 8,
        out_specs=(vmem,) * 4,
        scratch_shapes=[
            buf(128, 256),
            buf(4, 4, 2, 128, 256),
            buf(4, 2, 128, 256),
            buf(4, 256, 256),
            buf(4, 2, 128, 256),
            buf(4, 2, 128, 256),
            buf(2, 128, 256),
            buf(2, 128, 256),
            buf(4, 256, 256),
            buf(2, 128, 256),
            buf(2, 256, 256),
            buf(4, 4, 2, 128, 256),
            buf(4, 4, 128, 256),
            buf(4, 4, 128, 256),
            buf(4, 2, 64, 256),
            buf(4, 2, 128, 256),
            buf(4, 128, 256),
            buf(2, 64, 256),
            buf(2, 128, 256),
            buf(128, 256),
            pltpu.VMEM((128, 512), F32),
            pltpu.VMEM((16, 8, 128), F32),
            buf(128, 256),
            buf(128, 128),
            buf(128, 128),
            pltpu.VMEM((1, 128), jnp.int32),
            buf(128, 512),
            buf(4, 128),
            buf(128, 512),
            pltpu.SemaphoreType.DMA((N_COPIES,)),
            pltpu.SemaphoreType.DMA((N_COPIES,)),
            pltpu.SemaphoreType.DMA((N_LOADS,)),
        ],
        compiler_params=pltpu.CompilerParams(
            collective_id=0, has_side_effects=True, vmem_limit_bytes=63 * 2**20
        ),
    )(
        queries,
        keys,
        values,
        doc_start.reshape(1, 128),
        out_weight,
        residual,
        gain.reshape(4, 128),
        cotangent,
    )


def solution(mesh):
    placed = (
        P("dp", "tensor"),
        P("dp", None),
        P("dp", None),
        P("dp"),
        P("tensor", "dp"),
        P("dp", "tensor"),
        P("tensor"),
        P("dp", "tensor"),
    )
    return jax.shard_map(
        body,
        mesh=mesh,
        in_specs=placed,
        out_specs=(P("dp", "tensor"), P("dp", "tensor"), P("tensor", "dp"), P("dp", "tensor")),
        check_vma=False,
    )
```

```python
import functools
import math

import jax
import jax.numpy as jnp
from jax import lax
from jax.experimental import pallas as pl
from jax.experimental.pallas import tpu as pltpu
from jax.sharding import PartitionSpec as P

HD = 128
EPS = 1e-05
D_MODEL = 8192
MESH = pl.DeviceIdType.MESH
BF16 = jnp.bfloat16
F32 = jnp.float32
N_COPIES = 176
N_LOADS = 8


def kernel(
    queries_hbm,
    keys_hbm,
    values_hbm,
    starts_hbm,
    weight_hbm,
    residual_hbm,
    gain_hbm,
    cot_hbm,
    mixed,
    normed,
    grad_weight,
    grad_heads,
    mine,
    ho,
    ct,
    wt,
    s_y,
    z_in,
    q_sum,
    t_in,
    gw,
    gw_tr,
    gw_in,
    gp,
    g_in,
    gs,
    gx_tr,
    gx_in,
    gh,
    gz_tr,
    gz_in,
    g_own,
    stream,
    sq,
    queries,
    keys,
    values,
    starts_ref,
    residual,
    gain,
    cot,
    ssem,
    rsem,
    lsem,
):
    dp, tensor = lax.axis_index("dp"), lax.axis_index("tensor")
    zh, x, c = dp // 8, (dp // 2) % 4, dp % 2
    zl, y = tensor // 4, tensor % 4

    def dev(zh_, x_, c_, zl_, y_):
        return ((zh_ * 4 + x_) * 2 + c_, zl_ * 4 + y_)

    def plus(a, k):
        return (a + k) % 4

    y_dev = {k: dev(zh, x, c, zl, plus(y, k)) for k in (1, 3)}
    zl_dev = {k: dev(zh, x, c, plus(zl, k), y) for k in (1, 2, 3)}
    row_dev = {k: (dp, (tensor + k) % 16) for k in range(1, 16)}
    x_dev = {k: dev(zh, plus(x, k), c, zl, y) for k in (1, 3)}
    zh_dev = {k: dev(plus(zh, k), x, c, zl, y) for k in (1, 3)}
    sibling = dev(zh, x, 1 - c, zl, y)
    t_same, t_other = dev(zl, y, c, zh, x), dev(zl, y, 1 - c, zh, x)
    off_diagonal = (zh != zl) | (x != y)
    on_diagonal = (zh == zl) & (x == y)
    xy_dev = dev(zh, y, c, zl, x)
    xy_zh_dev = {k: dev(plus(zh, k), y, c, zl, x) for k in (1, 3)}

    kv = tensor // 2
    kv_cols = pl.ds(pl.multiple_of(kv * HD, HD), HD)
    loads = [
        pltpu.make_async_copy(src, dst, lsem.at[index])
        for index, (src, dst) in enumerate(
            (
                (cot_hbm, cot),
                (queries_hbm, queries),
                (keys_hbm.at[:, kv_cols], keys),
                (values_hbm.at[:, kv_cols], values),
                (starts_hbm, starts_ref),
                (weight_hbm, wt.at[y]),
                (residual_hbm, residual),
                (gain_hbm, gain),
            )
        )
    ]
    for load in loads:
        load.start()

    barrier = pltpu.get_barrier_semaphore()
    partners = [
        *row_dev.values(),
        *x_dev.values(),
        *zh_dev.values(),
        *xy_zh_dev.values(),
        sibling,
    ]
    for partner in partners:
        pl.semaphore_signal(barrier, inc=1, device_id=partner, device_id_type=MESH)

    @pl.when(off_diagonal)
    def _():
        for partner in (t_same, t_other):
            pl.semaphore_signal(barrier, inc=1, device_id=partner, device_id_type=MESH)

    @pl.when(x != y)
    def _():
        pl.semaphore_signal(barrier, inc=1, device_id=xy_dev, device_id_type=MESH)
        pl.semaphore_wait(barrier, len(partners) + 3)

    @pl.when((x == y) & (zh != zl))
    def _():
        pl.semaphore_wait(barrier, len(partners) + 2)

    @pl.when(on_diagonal)
    def _():
        pl.semaphore_wait(barrier, len(partners))

    for load in loads:
        load.wait()

    sent = []
    used = [0]

    def copy(src, dst, device):
        index = used[0]
        used[0] += 1
        return pltpu.make_async_remote_copy(
            src_ref=src,
            dst_ref=dst,
            send_sem=ssem.at[index],
            recv_sem=rsem.at[index],
            device_id=device,
            device_id_type=MESH,
        )

    def send(src, dst, device):
        made = copy(src, dst, device)
        made.start()
        sent.append(made)
        return made

    def transposed(own_src, other_src, dst):
        other = send(other_src, dst, t_other)
        same = copy(own_src, dst, t_same)

        @pl.when(off_diagonal)
        def _():
            same.start()

        @pl.when(on_diagonal)
        def _():
            dst[...] = own_src[...]

        def wait():
            other.wait_recv()

            @pl.when(off_diagonal)
            def _():
                same.wait()

        return wait

    def swapped(src, dst):
        made = copy(src, dst, xy_dev)

        @pl.when(x != y)
        def _():
            made.start()

        @pl.when(x == y)
        def _():
            dst[...] = src[...]

        def wait():
            @pl.when(x != y)
            def _():
                made.wait()

        return wait

    class Gather:
        def __init__(self, half, me, right, left, first=None):
            self.half, self.me, self.right, self.left = half, me, right, left
            src = dst = functools.partial(half, me)
            if first is not None:
                src, dst, right, left = first
            self.right0 = send(src(0), dst(0), right)
            self.left1 = send(src(1), dst(1), left)
            self.right1 = send(src(1), dst(1), right)
            self.left0 = send(src(0), dst(0), left)

        def forward(self):
            self.right0.wait_recv()
            half = self.half(plus(self.me, 3), 0)
            self.on_right = send(half, half, self.right)
            self.left1.wait_recv()
            half = self.half(plus(self.me, 1), 1)
            self.on_left = send(half, half, self.left)

        def neighbours(self):
            self.right1.wait_recv()
            self.left0.wait_recv()

        def finish(self):
            self.on_right.wait_recv()
            self.on_left.wait_recv()

    class Reduce:
        def __init__(self, half, tr, arrived, me, right, left, last=None):
            self.half, self.tr, self.arrived, self.me = half, tr, arrived, me
            last_right, last_left = (right, left) if last is None else last
            self.right, self.left = last_right, last_left
            opposite = plus(me, 2)
            self.t0 = send(half(opposite, 0), tr(0), right)
            self.t1 = send(half(opposite, 1), tr(1), left)
            self.r1 = send(half(plus(me, 1), 1), arrived(0, 1), last_right)
            self.l0 = send(half(plus(me, 3), 0), arrived(1, 0), last_left)

        def forward(self):
            self.t0.wait_recv()
            term = self.half(plus(self.me, 1), 0)
            term[...] = (term[...].astype(F32) + self.tr(0)[...].astype(F32)).astype(BF16)
            self.r0 = send(term, self.arrived(0, 0), self.right)
            self.t1.wait_recv()
            term = self.half(plus(self.me, 3), 1)
            term[...] = (term[...].astype(F32) + self.tr(1)[...].astype(F32)).astype(BF16)
            self.l1 = send(term, self.arrived(1, 1), self.left)

        def finish(self, h, own=None):
            own = self.half(self.me, h) if own is None else own
            (self.r0 if h == 0 else self.r1).wait_recv()
            (self.l0 if h == 0 else self.l1).wait_recv()
            return (
                own[...].astype(F32)
                + self.arrived(0, h)[...].astype(F32)
                + self.arrived(1, h)[...].astype(F32)
            )

    def cot_half(k):
        return cot.at[:, pl.ds(pl.multiple_of(k * 256, 256), 256)]

    w_y = Gather(lambda o, h: wt.at[o, pl.ds(h * 128, 128)], y, y_dev[1], y_dev[3])

    key_rows, value_rows = keys[...], values[...]
    starts = jnp.broadcast_to(starts_ref[...] - dp * 128, (128, 128)).T
    row = lax.broadcasted_iota(jnp.int32, (128, 128), 0)
    col = lax.broadcasted_iota(jnp.int32, (128, 128), 1)
    allowed = (col >= starts) & (col <= row)
    for head in range(2):
        scores = lax.dot_general(
            queries[:, head * HD : (head + 1) * HD],
            key_rows,
            (((1,), (1,)), ((), ())),
            preferred_element_type=F32,
        ) / math.sqrt(HD)
        scores = jnp.where(allowed, scores, -1e30)
        top = jnp.max(scores, axis=-1, keepdims=True)
        weights = jnp.where(allowed, jnp.exp(scores - top), 0.0)
        probs = (weights / jnp.sum(weights, axis=-1, keepdims=True)).astype(BF16)
        mine[:, head * HD : (head + 1) * HD] = jnp.dot(
            probs, value_rows, preferred_element_type=F32
        ).astype(BF16)

    def rows64(h):
        return pl.ds(h * 64, 64)

    def ho_x(g):
        return Gather(lambda o, h: ho.at[g, o, c, rows64(h)], x, x_dev[1], x_dev[3])

    def ho_core(g):
        return send(ho.at[g, :, c], ho.at[g, :, c], sibling)

    z_base = used[0]
    used[0] += 4

    def z_copy(k, src):
        return pltpu.make_async_remote_copy(
            src_ref=src,
            dst_ref=z_in.at[k],
            send_sem=ssem.at[z_base + k],
            recv_sem=rsem.at[z_base + k],
            device_id=dev(zh, x, c, plus(zl, k), y),
            device_id_type=MESH,
        )

    def project(g):
        part = jnp.dot(ho[g, 0].reshape(256, 256), wt[0], preferred_element_type=F32)
        for i in range(1, 4):
            part = part + jnp.dot(
                ho[g, i].reshape(256, 256), wt[i], preferred_element_type=F32
            )
        s_y[g] = part.astype(BF16).reshape(2, 128, 256)
        k = plus(g, 4 - zl)

        @pl.when(k != 0)
        def _():
            z_copy(k, s_y.at[g]).start()

    def heads_grad(g):
        def tile(i, carry):
            gp[g, i] = (
                lax.dot_general(
                    ct[g].reshape(256, 256),
                    wt[i],
                    (((1,), (1,)), ((), ())),
                    preferred_element_type=F32,
                )
                .astype(BF16)
                .reshape(2, 128, 256)
            )
            return carry

        lax.fori_loop(0, 4, tile, 0)
        return send(gp.at[g, :, 1 - c], g_in.at[g], sibling)

    def heads_x(g, from_core):
        from_core.wait_recv()

        def tile(i, carry):
            gs[g, i] = (gp[g, i, c].astype(F32) + g_in[g, i].astype(F32)).astype(BF16)
            return carry

        lax.fori_loop(0, 4, tile, 0)
        return Reduce(
            lambda o, h: gs.at[g, o, rows64(h)],
            lambda h: gx_tr.at[g, h],
            lambda side, h: gx_in.at[g, side, rows64(h)],
            x,
            x_dev[1],
            x_dev[3],
        )

    ho_z = Gather(
        lambda o, h: ho.at[o, x, c, rows64(h)],
        zh,
        zh_dev[1],
        zh_dev[3],
        (
            lambda h: mine.at[rows64(h)],
            lambda h: ho.at[zh, y, c, rows64(h)],
            xy_zh_dev[1],
            xy_zh_dev[3],
        ),
    )
    mine_wait = swapped(mine, ho.at[zh, y, c])
    cot_wait = transposed(cot_half(c), cot_half(1 - c), ct.at[zh, c])
    groups = [zh, plus(zh, 3), plus(zh, 1), plus(zh, 2)]
    cgroups = [zl, plus(zl, 3), plus(zl, 2), plus(zl, 1)]
    w_y.forward()
    mine_wait()
    hx = [ho_x(groups[0])]
    ho_z.forward()
    hx[0].forward()
    w_y.neighbours()
    w_y.finish()
    ho_z.neighbours()
    hx.append(ho_x(groups[1]))
    hx.append(ho_x(groups[2]))
    cot_wait()
    ct_zl = [send(ct.at[zl], ct.at[zl], zl_dev[k]) for k in (1, 2, 3)]
    gc = [heads_grad(cgroups[0])]
    hx[0].neighbours()
    hx[0].finish()
    hc = [ho_core(groups[0])]
    gx = [heads_x(cgroups[0], gc[0])]
    hc[0].wait_recv()
    project(groups[0])
    hx[1].forward()
    hx[2].forward()
    ho_z.finish()
    hx.append(ho_x(groups[3]))
    for k in (1, 2):
        hx[k].neighbours()
        hx[k].finish()
        hc.append(ho_core(groups[k]))
    for k in (1, 2, 3):
        ct_zl[k - 1].wait_recv()
        gc.append(heads_grad(cgroups[k]))
        if k < 3:
            hc[k].wait_recv()
            project(groups[k])
    hx[3].forward()
    for k in (1, 2, 3):
        gx.append(heads_x(cgroups[k], gc[k]))
    gx[0].forward()
    hx[3].neighbours()
    hx[3].finish()
    hc.append(ho_core(groups[3]))
    hc[3].wait_recv()
    project(groups[3])
    for k in (1, 2, 3):
        gx[k].forward()
    for k in range(4):
        for h in range(2):
            gh[cgroups[k], rows64(h)] = gx[k].finish(h).astype(BF16)
    gz = Reduce(
        lambda o, h: gh.at[o, rows64(h)],
        lambda h: gz_tr.at[h],
        lambda side, h: gz_in.at[side, rows64(h)],
        zh,
        zh_dev[1],
        zh_dev[3],
        (xy_zh_dev[1], xy_zh_dev[3]),
    )
    own_wait = swapped(gh.at[zh], g_own)

    for k in (1, 2, 3):
        z_copy(k, s_y.at[0]).wait_recv()
    for h in range(2):
        q_sum[h] = (
            s_y[zl, h].astype(F32)
            + z_in[1, h].astype(F32)
            + z_in[2, h].astype(F32)
            + z_in[3, h].astype(F32)
        ).astype(BF16)
    p_wait = transposed(q_sum.at[c], q_sum.at[1 - c], t_in.at[c])

    def weight_tile(i, carry):
        part = jnp.zeros((256, 256), F32)
        for g in range(4):
            part = part + lax.dot_general(
                ho[g, i].reshape(256, 256),
                ct[g].reshape(256, 256),
                (((0,), (0,)), ((), ())),
                preferred_element_type=F32,
            )
        gw[i] = part.astype(BF16)
        return carry

    lax.fori_loop(0, 4, weight_tile, 0)
    gw_y = Reduce(
        lambda o, h: gw.at[o, pl.ds(h * 128, 128)],
        lambda h: gw_tr.at[h],
        lambda side, h: gw_in.at[side, pl.ds(h * 128, 128)],
        y,
        y_dev[1],
        y_dev[3],
    )
    gz.forward()
    gw_y.forward()

    p_wait()
    squares = jnp.zeros((128, 1), F32)
    for k in range(2):
        cols = slice(k * 256, (k + 1) * 256)
        part = residual[:, cols].astype(F32) + t_in[k].astype(F32)
        stream[:, cols] = part
        mixed[:, cols] = part.astype(BF16)
        squares = squares + jnp.sum(part * part, axis=1, keepdims=True)
    sq[0] = jnp.broadcast_to(squares, (128, 128)).T[:8]
    norms = [send(sq.at[0], sq.at[k], row_dev[k]) for k in range(1, 16)]

    for h in range(2):
        grad_weight[h * 128 : (h + 1) * 128, :] = gw_y.finish(h).astype(BF16)
    own_wait()
    for h in range(2):
        rows = g_own.at[rows64(h)]
        grad_heads[h * 64 : (h + 1) * 64, :] = gz.finish(h, rows).astype(BF16)

    for made in norms:
        made.wait_recv()
    total = jnp.sum(sq[...], axis=0)
    mean_square = jnp.broadcast_to(total[:1], (128, 128)).T[:, :1] / D_MODEL
    factor = lax.rsqrt(mean_square + EPS)
    for k in range(4):
        cols = slice(k * 128, (k + 1) * 128)
        normed[:, cols] = (stream[:, cols] * factor * gain[k : k + 1, :].astype(F32)).astype(BF16)

    for made in sent:
        made.wait_send()
    for k in (1, 2, 3):
        z_copy(k, s_y.at[0]).wait_send()


def copy_results(*refs):
    sources, results, held = refs[:4], refs[4:8], refs[8:12]
    in_sem, out_sem = refs[12:]
    loads = [pltpu.make_async_copy(sources[k], held[k], in_sem.at[k]) for k in range(4)]
    stores = [pltpu.make_async_copy(held[k], results[k], out_sem.at[k]) for k in range(4)]
    for load in loads:
        load.start()
    for load, store in zip(loads, stores):
        load.wait()
        store.start()
    for store in stores:
        store.wait()


def body(queries, keys, values, doc_start, out_weight, residual, gain, cotangent):
    vmem = pl.BlockSpec(memory_space=pltpu.VMEM)

    def buf(*shape):
        return pltpu.VMEM(shape, BF16)

    sizes = ((128, 512), (128, 512), (256, 256), (128, 256))
    shapes = tuple(jax.ShapeDtypeStruct(size, BF16) for size in sizes)
    results = pl.pallas_call(
        kernel,
        out_shape=shapes,
        in_specs=[pl.BlockSpec(memory_space=pltpu.HBM)] * 8,
        out_specs=(vmem,) * 4,
        scratch_shapes=[
            buf(128, 256),
            buf(4, 4, 2, 128, 256),
            buf(4, 2, 128, 256),
            buf(4, 256, 256),
            buf(4, 2, 128, 256),
            buf(4, 2, 128, 256),
            buf(2, 128, 256),
            buf(2, 128, 256),
            buf(4, 256, 256),
            buf(2, 128, 256),
            buf(2, 256, 256),
            buf(4, 4, 2, 128, 256),
            buf(4, 4, 128, 256),
            buf(4, 4, 128, 256),
            buf(4, 2, 64, 256),
            buf(4, 2, 128, 256),
            buf(4, 128, 256),
            buf(2, 64, 256),
            buf(2, 128, 256),
            buf(128, 256),
            pltpu.VMEM((128, 512), F32),
            pltpu.VMEM((16, 8, 128), F32),
            buf(128, 256),
            buf(128, 128),
            buf(128, 128),
            pltpu.VMEM((1, 128), jnp.int32),
            buf(128, 512),
            buf(4, 128),
            buf(128, 512),
            pltpu.SemaphoreType.DMA((N_COPIES,)),
            pltpu.SemaphoreType.DMA((N_COPIES,)),
            pltpu.SemaphoreType.DMA((N_LOADS,)),
        ],
        compiler_params=pltpu.CompilerParams(
            collective_id=0, has_side_effects=True, vmem_limit_bytes=63 * 2**20
        ),
    )(
        queries,
        keys,
        values,
        doc_start.reshape(1, 128),
        out_weight,
        residual,
        gain.reshape(4, 128),
        cotangent,
    )
    hbm = pl.BlockSpec(memory_space=pltpu.HBM)
    return pl.pallas_call(
        copy_results,
        out_shape=shapes,
        in_specs=[hbm] * 4,
        out_specs=(hbm,) * 4,
        scratch_shapes=[
            *(buf(*size) for size in sizes),
            pltpu.SemaphoreType.DMA((4,)),
            pltpu.SemaphoreType.DMA((4,)),
        ],
        compiler_params=pltpu.CompilerParams(vmem_limit_bytes=63 * 2**20),
    )(*results)


def solution(mesh):
    placed = (
        P("dp", "tensor"),
        P("dp", None),
        P("dp", None),
        P("dp"),
        P("tensor", "dp"),
        P("dp", "tensor"),
        P("tensor"),
        P("dp", "tensor"),
    )
    return jax.shard_map(
        body,
        mesh=mesh,
        in_specs=placed,
        out_specs=(P("dp", "tensor"), P("dp", "tensor"), P("tensor", "dp"), P("dp", "tensor")),
        check_vma=False,
    )
```

```python
import functools
import math

import jax
import jax.numpy as jnp
from jax import lax
from jax.experimental import pallas as pl
from jax.experimental.pallas import tpu as pltpu
from jax.sharding import PartitionSpec as P

HD = 128
EPS = 1e-05
D_MODEL = 8192
MESH = pl.DeviceIdType.MESH
BF16 = jnp.bfloat16
F32 = jnp.float32
N_COPIES = 176
N_LOADS = 8


def kernel(
    queries_hbm,
    keys_hbm,
    values_hbm,
    starts_hbm,
    weight_hbm,
    residual_hbm,
    gain_hbm,
    cot_hbm,
    mixed,
    normed,
    grad_weight,
    grad_heads,
    mine,
    ho,
    ct,
    wt,
    s_y,
    z_in,
    q_sum,
    t_in,
    gw,
    gw_tr,
    gw_in,
    gp,
    g_in,
    gs,
    gx_tr,
    gx_in,
    gh,
    gz_tr,
    gz_in,
    g_own,
    stream,
    sq,
    queries,
    keys,
    values,
    starts_ref,
    residual,
    gain,
    cot,
    ssem,
    rsem,
    lsem,
):
    dp, tensor = lax.axis_index("dp"), lax.axis_index("tensor")
    zh, x, c = dp // 8, (dp // 2) % 4, dp % 2
    zl, y = tensor // 4, tensor % 4

    def dev(zh_, x_, c_, zl_, y_):
        return ((zh_ * 4 + x_) * 2 + c_, zl_ * 4 + y_)

    def plus(a, k):
        return (a + k) % 4

    y_dev = {k: dev(zh, x, c, zl, plus(y, k)) for k in (1, 3)}
    zl_dev = {k: dev(zh, x, c, plus(zl, k), y) for k in (1, 2, 3)}
    row_dev = {k: (dp, (tensor + k) % 16) for k in range(1, 16)}
    x_dev = {k: dev(zh, plus(x, k), c, zl, y) for k in (1, 2, 3)}
    zh_dev = {k: dev(plus(zh, k), x, c, zl, y) for k in (1, 3)}
    sibling = dev(zh, x, 1 - c, zl, y)
    t_same, t_other = dev(zl, y, c, zh, x), dev(zl, y, 1 - c, zh, x)
    off_diagonal = (zh != zl) | (x != y)
    on_diagonal = (zh == zl) & (x == y)
    xy_dev = dev(zh, y, c, zl, x)
    xy_zh_dev = {k: dev(plus(zh, k), y, c, zl, x) for k in (1, 3)}

    kv = tensor // 2
    kv_cols = pl.ds(pl.multiple_of(kv * HD, HD), HD)
    loads = [
        pltpu.make_async_copy(src, dst, lsem.at[index])
        for index, (src, dst) in enumerate(
            (
                (cot_hbm, cot),
                (queries_hbm, queries),
                (keys_hbm.at[:, kv_cols], keys),
                (values_hbm.at[:, kv_cols], values),
                (starts_hbm, starts_ref),
                (weight_hbm, wt.at[y]),
                (residual_hbm, residual),
                (gain_hbm, gain),
            )
        )
    ]
    for load in loads:
        load.start()

    barrier = pltpu.get_barrier_semaphore()
    partners = [
        *row_dev.values(),
        *x_dev.values(),
        *zh_dev.values(),
        *xy_zh_dev.values(),
        sibling,
    ]
    for partner in partners:
        pl.semaphore_signal(barrier, inc=1, device_id=partner, device_id_type=MESH)

    @pl.when(off_diagonal)
    def _():
        for partner in (t_same, t_other):
            pl.semaphore_signal(barrier, inc=1, device_id=partner, device_id_type=MESH)

    @pl.when(x != y)
    def _():
        pl.semaphore_signal(barrier, inc=1, device_id=xy_dev, device_id_type=MESH)
        pl.semaphore_wait(barrier, len(partners) + 3)

    @pl.when((x == y) & (zh != zl))
    def _():
        pl.semaphore_wait(barrier, len(partners) + 2)

    @pl.when(on_diagonal)
    def _():
        pl.semaphore_wait(barrier, len(partners))

    for load in loads:
        load.wait()

    sent = []
    used = [0]

    def copy(src, dst, device):
        index = used[0]
        used[0] += 1
        return pltpu.make_async_remote_copy(
            src_ref=src,
            dst_ref=dst,
            send_sem=ssem.at[index],
            recv_sem=rsem.at[index],
            device_id=device,
            device_id_type=MESH,
        )

    def send(src, dst, device):
        made = copy(src, dst, device)
        made.start()
        sent.append(made)
        return made

    def transposed(own_src, other_src, dst):
        other = send(other_src, dst, t_other)
        same = copy(own_src, dst, t_same)

        @pl.when(off_diagonal)
        def _():
            same.start()

        @pl.when(on_diagonal)
        def _():
            dst[...] = own_src[...]

        def wait():
            other.wait_recv()

            @pl.when(off_diagonal)
            def _():
                same.wait()

        return wait

    def swapped(src, dst):
        made = copy(src, dst, xy_dev)

        @pl.when(x != y)
        def _():
            made.start()

        @pl.when(x == y)
        def _():
            dst[...] = src[...]

        def wait():
            @pl.when(x != y)
            def _():
                made.wait()

        return wait

    class Gather:
        def __init__(self, half, me, right, left, first=None):
            self.half, self.me, self.right, self.left = half, me, right, left
            src = dst = functools.partial(half, me)
            if first is not None:
                src, dst, right, left = first
            self.right0 = send(src(0), dst(0), right)
            self.left1 = send(src(1), dst(1), left)
            self.right1 = send(src(1), dst(1), right)
            self.left0 = send(src(0), dst(0), left)

        def forward(self):
            self.right0.wait_recv()
            half = self.half(plus(self.me, 3), 0)
            self.on_right = send(half, half, self.right)
            self.left1.wait_recv()
            half = self.half(plus(self.me, 1), 1)
            self.on_left = send(half, half, self.left)

        def neighbours(self):
            self.right1.wait_recv()
            self.left0.wait_recv()

        def finish(self):
            self.on_right.wait_recv()
            self.on_left.wait_recv()

    class Reduce:
        def __init__(self, half, tr, arrived, me, right, left, last=None):
            self.half, self.tr, self.arrived, self.me = half, tr, arrived, me
            last_right, last_left = (right, left) if last is None else last
            self.right, self.left = last_right, last_left
            opposite = plus(me, 2)
            self.t0 = send(half(opposite, 0), tr(0), right)
            self.t1 = send(half(opposite, 1), tr(1), left)
            self.r1 = send(half(plus(me, 1), 1), arrived(0, 1), last_right)
            self.l0 = send(half(plus(me, 3), 0), arrived(1, 0), last_left)

        def forward(self):
            self.t0.wait_recv()
            term = self.half(plus(self.me, 1), 0)
            term[...] = (term[...].astype(F32) + self.tr(0)[...].astype(F32)).astype(BF16)
            self.r0 = send(term, self.arrived(0, 0), self.right)
            self.t1.wait_recv()
            term = self.half(plus(self.me, 3), 1)
            term[...] = (term[...].astype(F32) + self.tr(1)[...].astype(F32)).astype(BF16)
            self.l1 = send(term, self.arrived(1, 1), self.left)

        def finish(self, h, own=None):
            own = self.half(self.me, h) if own is None else own
            (self.r0 if h == 0 else self.r1).wait_recv()
            (self.l0 if h == 0 else self.l1).wait_recv()
            return (
                own[...].astype(F32)
                + self.arrived(0, h)[...].astype(F32)
                + self.arrived(1, h)[...].astype(F32)
            )

    def cot_half(k):
        return cot.at[:, pl.ds(pl.multiple_of(k * 256, 256), 256)]

    w_y = Gather(lambda o, h: wt.at[o, pl.ds(h * 128, 128)], y, y_dev[1], y_dev[3])

    key_rows, value_rows = keys[...], values[...]
    starts = jnp.broadcast_to(starts_ref[...] - dp * 128, (128, 128)).T
    row = lax.broadcasted_iota(jnp.int32, (128, 128), 0)
    col = lax.broadcasted_iota(jnp.int32, (128, 128), 1)
    allowed = (col >= starts) & (col <= row)
    for head in range(2):
        scores = lax.dot_general(
            queries[:, head * HD : (head + 1) * HD],
            key_rows,
            (((1,), (1,)), ((), ())),
            preferred_element_type=F32,
        ) / math.sqrt(HD)
        scores = jnp.where(allowed, scores, -1e30)
        top = jnp.max(scores, axis=-1, keepdims=True)
        weights = jnp.where(allowed, jnp.exp(scores - top), 0.0)
        probs = (weights / jnp.sum(weights, axis=-1, keepdims=True)).astype(BF16)
        mine[:, head * HD : (head + 1) * HD] = jnp.dot(
            probs, value_rows, preferred_element_type=F32
        ).astype(BF16)

    def rows64(h):
        return pl.ds(h * 64, 64)

    def ho_x(g):
        return Gather(lambda o, h: ho.at[g, o, c, rows64(h)], x, x_dev[1], x_dev[3])

    def ho_core(g):
        return send(ho.at[g, :, c], ho.at[g, :, c], sibling)

    z_base = used[0]
    used[0] += 4

    def z_copy(k, src):
        return pltpu.make_async_remote_copy(
            src_ref=src,
            dst_ref=z_in.at[k],
            send_sem=ssem.at[z_base + k],
            recv_sem=rsem.at[z_base + k],
            device_id=dev(zh, x, c, plus(zl, k), y),
            device_id_type=MESH,
        )

    def project(g):
        part = jnp.dot(ho[g, 0].reshape(256, 256), wt[0], preferred_element_type=F32)
        for i in range(1, 4):
            part = part + jnp.dot(
                ho[g, i].reshape(256, 256), wt[i], preferred_element_type=F32
            )
        s_y[g] = part.astype(BF16).reshape(2, 128, 256)
        k = plus(g, 4 - zl)

        @pl.when(k != 0)
        def _():
            z_copy(k, s_y.at[g]).start()

    def heads_grad(g):
        def tile(i, carry):
            gp[g, i] = (
                lax.dot_general(
                    ct[g].reshape(256, 256),
                    wt[i],
                    (((1,), (1,)), ((), ())),
                    preferred_element_type=F32,
                )
                .astype(BF16)
                .reshape(2, 128, 256)
            )
            return carry

        lax.fori_loop(0, 4, tile, 0)
        return send(gp.at[g, :, 1 - c], g_in.at[g], sibling)

    def heads_x(g, from_core):
        from_core.wait_recv()

        def tile(i, carry):
            gs[g, i] = (gp[g, i, c].astype(F32) + g_in[g, i].astype(F32)).astype(BF16)
            return carry

        lax.fori_loop(0, 4, tile, 0)
        return Reduce(
            lambda o, h: gs.at[g, o, rows64(h)],
            lambda h: gx_tr.at[g, h],
            lambda side, h: gx_in.at[g, side, rows64(h)],
            x,
            x_dev[1],
            x_dev[3],
        )

    ho_z = Gather(
        lambda o, h: ho.at[o, x, c, rows64(h)],
        zh,
        zh_dev[1],
        zh_dev[3],
        (
            lambda h: mine.at[rows64(h)],
            lambda h: ho.at[zh, y, c, rows64(h)],
            xy_zh_dev[1],
            xy_zh_dev[3],
        ),
    )
    mine_wait = swapped(mine, ho.at[zh, y, c])
    cot_wait = transposed(cot_half(c), cot_half(1 - c), ct.at[zh, c])
    groups = [zh, plus(zh, 3), plus(zh, 1), plus(zh, 2)]
    cgroups = [zl, plus(zl, 3), plus(zl, 2), plus(zl, 1)]
    w_y.forward()
    mine_wait()
    hx = [ho_x(groups[0])]
    ho_z.forward()
    hx[0].forward()
    w_y.neighbours()
    w_y.finish()
    ho_z.neighbours()
    hx.append(ho_x(groups[1]))
    hx.append(ho_x(groups[2]))
    cot_wait()
    ct_zl = [send(ct.at[zl], ct.at[zl], zl_dev[k]) for k in (1, 2, 3)]
    gc = [heads_grad(cgroups[0])]
    hx[0].neighbours()
    hx[0].finish()
    hc = [ho_core(groups[0])]
    gx = [heads_x(cgroups[0], gc[0])]
    hc[0].wait_recv()
    project(groups[0])
    hx[1].forward()
    hx[2].forward()
    ho_z.finish()
    last = ho.at[groups[3], x, c]
    hx_last = [send(last, last, x_dev[k]) for k in (1, 3, 2)]
    for k in (1, 2):
        hx[k].neighbours()
        hx[k].finish()
        hc.append(ho_core(groups[k]))
    for k in (1, 2, 3):
        ct_zl[k - 1].wait_recv()
        gc.append(heads_grad(cgroups[k]))
        if k < 3:
            hc[k].wait_recv()
            project(groups[k])
    for k in (1, 2, 3):
        gx.append(heads_x(cgroups[k], gc[k]))
    gx[0].forward()
    for made in hx_last:
        made.wait_recv()
    hc.append(ho_core(groups[3]))
    hc[3].wait_recv()
    project(groups[3])
    for k in (1, 2, 3):
        gx[k].forward()
    for k in range(4):
        for h in range(2):
            gh[cgroups[k], rows64(h)] = gx[k].finish(h).astype(BF16)
    gz = Reduce(
        lambda o, h: gh.at[o, rows64(h)],
        lambda h: gz_tr.at[h],
        lambda side, h: gz_in.at[side, rows64(h)],
        zh,
        zh_dev[1],
        zh_dev[3],
        (xy_zh_dev[1], xy_zh_dev[3]),
    )
    own_wait = swapped(gh.at[zh], g_own)

    for k in (1, 2, 3):
        z_copy(k, s_y.at[0]).wait_recv()
    for h in range(2):
        q_sum[h] = (
            s_y[zl, h].astype(F32)
            + z_in[1, h].astype(F32)
            + z_in[2, h].astype(F32)
            + z_in[3, h].astype(F32)
        ).astype(BF16)
    p_wait = transposed(q_sum.at[c], q_sum.at[1 - c], t_in.at[c])

    def weight_tile(i, carry):
        part = jnp.zeros((256, 256), F32)
        for g in range(4):
            part = part + lax.dot_general(
                ho[g, i].reshape(256, 256),
                ct[g].reshape(256, 256),
                (((0,), (0,)), ((), ())),
                preferred_element_type=F32,
            )
        gw[i] = part.astype(BF16)
        return carry

    lax.fori_loop(0, 4, weight_tile, 0)
    gw_y = Reduce(
        lambda o, h: gw.at[o, pl.ds(h * 128, 128)],
        lambda h: gw_tr.at[h],
        lambda side, h: gw_in.at[side, pl.ds(h * 128, 128)],
        y,
        y_dev[1],
        y_dev[3],
    )
    gz.forward()
    gw_y.forward()

    p_wait()
    squares = jnp.zeros((128, 1), F32)
    for k in range(2):
        cols = slice(k * 256, (k + 1) * 256)
        part = residual[:, cols].astype(F32) + t_in[k].astype(F32)
        stream[:, cols] = part
        mixed[:, cols] = part.astype(BF16)
        squares = squares + jnp.sum(part * part, axis=1, keepdims=True)
    sq[0] = jnp.broadcast_to(squares, (128, 128)).T[:8]
    norms = [send(sq.at[0], sq.at[k], row_dev[k]) for k in range(1, 16)]

    for h in range(2):
        grad_weight[h * 128 : (h + 1) * 128, :] = gw_y.finish(h).astype(BF16)
    own_wait()
    for h in range(2):
        rows = g_own.at[rows64(h)]
        grad_heads[h * 64 : (h + 1) * 64, :] = gz.finish(h, rows).astype(BF16)

    for made in norms:
        made.wait_recv()
    total = jnp.sum(sq[...], axis=0)
    mean_square = jnp.broadcast_to(total[:1], (128, 128)).T[:, :1] / D_MODEL
    factor = lax.rsqrt(mean_square + EPS)
    for k in range(4):
        cols = slice(k * 128, (k + 1) * 128)
        normed[:, cols] = (stream[:, cols] * factor * gain[k : k + 1, :].astype(F32)).astype(BF16)

    for made in sent:
        made.wait_send()
    for k in (1, 2, 3):
        z_copy(k, s_y.at[0]).wait_send()


def copy_results(*refs):
    sources, results, held = refs[:4], refs[4:8], refs[8:12]
    in_sem, out_sem = refs[12:]
    loads = [pltpu.make_async_copy(sources[k], held[k], in_sem.at[k]) for k in range(4)]
    stores = [pltpu.make_async_copy(held[k], results[k], out_sem.at[k]) for k in range(4)]
    for load in loads:
        load.start()
    for load, store in zip(loads, stores):
        load.wait()
        store.start()
    for store in stores:
        store.wait()


def body(queries, keys, values, doc_start, out_weight, residual, gain, cotangent):
    vmem = pl.BlockSpec(memory_space=pltpu.VMEM)

    def buf(*shape):
        return pltpu.VMEM(shape, BF16)

    sizes = ((128, 512), (128, 512), (256, 256), (128, 256))
    shapes = tuple(jax.ShapeDtypeStruct(size, BF16) for size in sizes)
    results = pl.pallas_call(
        kernel,
        out_shape=shapes,
        in_specs=[pl.BlockSpec(memory_space=pltpu.HBM)] * 8,
        out_specs=(vmem,) * 4,
        scratch_shapes=[
            buf(128, 256),
            buf(4, 4, 2, 128, 256),
            buf(4, 2, 128, 256),
            buf(4, 256, 256),
            buf(4, 2, 128, 256),
            buf(4, 2, 128, 256),
            buf(2, 128, 256),
            buf(2, 128, 256),
            buf(4, 256, 256),
            buf(2, 128, 256),
            buf(2, 256, 256),
            buf(4, 4, 2, 128, 256),
            buf(4, 4, 128, 256),
            buf(4, 4, 128, 256),
            buf(4, 2, 64, 256),
            buf(4, 2, 128, 256),
            buf(4, 128, 256),
            buf(2, 64, 256),
            buf(2, 128, 256),
            buf(128, 256),
            pltpu.VMEM((128, 512), F32),
            pltpu.VMEM((16, 8, 128), F32),
            buf(128, 256),
            buf(128, 128),
            buf(128, 128),
            pltpu.VMEM((1, 128), jnp.int32),
            buf(128, 512),
            buf(4, 128),
            buf(128, 512),
            pltpu.SemaphoreType.DMA((N_COPIES,)),
            pltpu.SemaphoreType.DMA((N_COPIES,)),
            pltpu.SemaphoreType.DMA((N_LOADS,)),
        ],
        compiler_params=pltpu.CompilerParams(
            collective_id=0, has_side_effects=True, vmem_limit_bytes=63 * 2**20
        ),
    )(
        queries,
        keys,
        values,
        doc_start.reshape(1, 128),
        out_weight,
        residual,
        gain.reshape(4, 128),
        cotangent,
    )
    hbm = pl.BlockSpec(memory_space=pltpu.HBM)
    return pl.pallas_call(
        copy_results,
        out_shape=shapes,
        in_specs=[hbm] * 4,
        out_specs=(hbm,) * 4,
        scratch_shapes=[
            *(buf(*size) for size in sizes),
            pltpu.SemaphoreType.DMA((4,)),
            pltpu.SemaphoreType.DMA((4,)),
        ],
        compiler_params=pltpu.CompilerParams(vmem_limit_bytes=63 * 2**20),
    )(*results)


def solution(mesh):
    placed = (
        P("dp", "tensor"),
        P("dp", None),
        P("dp", None),
        P("dp"),
        P("tensor", "dp"),
        P("dp", "tensor"),
        P("tensor"),
        P("dp", "tensor"),
    )
    return jax.shard_map(
        body,
        mesh=mesh,
        in_specs=placed,
        out_specs=(P("dp", "tensor"), P("dp", "tensor"), P("tensor", "dp"), P("dp", "tensor")),
        check_vma=False,
    )
```

```python
import functools
import math

import jax
import jax.numpy as jnp
from jax import lax
from jax.experimental import pallas as pl
from jax.experimental.pallas import tpu as pltpu
from jax.sharding import PartitionSpec as P

HD = 128
EPS = 1e-05
D_MODEL = 8192
MESH = pl.DeviceIdType.MESH
BF16 = jnp.bfloat16
F32 = jnp.float32
N_COPIES = 176
N_LOADS = 8


def kernel(
    queries_hbm,
    keys_hbm,
    values_hbm,
    starts_hbm,
    weight_hbm,
    residual_hbm,
    gain_hbm,
    cot_hbm,
    mixed,
    normed,
    grad_weight,
    grad_heads,
    mine,
    ho,
    ct,
    wt,
    s_y,
    z_in,
    q_sum,
    t_in,
    gw,
    gw_tr,
    gw_in,
    gp,
    g_in,
    gs,
    gx_tr,
    gx_in,
    gh,
    gz_tr,
    gz_in,
    g_own,
    stream,
    sq,
    queries,
    keys,
    values,
    starts_ref,
    residual,
    gain,
    cot,
    ssem,
    rsem,
    lsem,
):
    dp, tensor = lax.axis_index("dp"), lax.axis_index("tensor")
    zh, x, c = dp // 8, (dp // 2) % 4, dp % 2
    zl, y = tensor // 4, tensor % 4

    def dev(zh_, x_, c_, zl_, y_):
        return ((zh_ * 4 + x_) * 2 + c_, zl_ * 4 + y_)

    def plus(a, k):
        return (a + k) % 4

    y_dev = {k: dev(zh, x, c, zl, plus(y, k)) for k in (1, 3)}
    zl_dev = {k: dev(zh, x, c, plus(zl, k), y) for k in (1, 2, 3)}
    row_dev = {k: (dp, (tensor + k) % 16) for k in range(1, 16)}
    x_dev = {k: dev(zh, plus(x, k), c, zl, y) for k in (1, 2, 3)}
    zh_dev = {k: dev(plus(zh, k), x, c, zl, y) for k in (1, 3)}
    sibling = dev(zh, x, 1 - c, zl, y)
    t_same, t_other = dev(zl, y, c, zh, x), dev(zl, y, 1 - c, zh, x)
    off_diagonal = (zh != zl) | (x != y)
    on_diagonal = (zh == zl) & (x == y)
    xy_dev = dev(zh, y, c, zl, x)
    xy_zh_dev = {k: dev(plus(zh, k), y, c, zl, x) for k in (1, 3)}

    kv = tensor // 2
    kv_cols = pl.ds(pl.multiple_of(kv * HD, HD), HD)
    loads = [
        pltpu.make_async_copy(src, dst, lsem.at[index])
        for index, (src, dst) in enumerate(
            (
                (cot_hbm, cot),
                (queries_hbm, queries),
                (keys_hbm.at[:, kv_cols], keys),
                (values_hbm.at[:, kv_cols], values),
                (starts_hbm, starts_ref),
                (weight_hbm, wt.at[y]),
                (residual_hbm, residual),
                (gain_hbm, gain),
            )
        )
    ]
    for load in loads:
        load.start()

    barrier = pltpu.get_barrier_semaphore()
    partners = [
        *row_dev.values(),
        *x_dev.values(),
        *zh_dev.values(),
        *xy_zh_dev.values(),
        sibling,
    ]
    for partner in partners:
        pl.semaphore_signal(barrier, inc=1, device_id=partner, device_id_type=MESH)

    @pl.when(off_diagonal)
    def _():
        for partner in (t_same, t_other):
            pl.semaphore_signal(barrier, inc=1, device_id=partner, device_id_type=MESH)

    @pl.when(x != y)
    def _():
        pl.semaphore_signal(barrier, inc=1, device_id=xy_dev, device_id_type=MESH)
        pl.semaphore_wait(barrier, len(partners) + 3)

    @pl.when((x == y) & (zh != zl))
    def _():
        pl.semaphore_wait(barrier, len(partners) + 2)

    @pl.when(on_diagonal)
    def _():
        pl.semaphore_wait(barrier, len(partners))

    for load in loads:
        load.wait()

    sent = []
    used = [0]

    def copy(src, dst, device):
        index = used[0]
        used[0] += 1
        return pltpu.make_async_remote_copy(
            src_ref=src,
            dst_ref=dst,
            send_sem=ssem.at[index],
            recv_sem=rsem.at[index],
            device_id=device,
            device_id_type=MESH,
        )

    def send(src, dst, device):
        made = copy(src, dst, device)
        made.start()
        sent.append(made)
        return made

    def transposed(own_src, other_src, dst):
        other = send(other_src, dst, t_other)
        same = copy(own_src, dst, t_same)

        @pl.when(off_diagonal)
        def _():
            same.start()

        @pl.when(on_diagonal)
        def _():
            dst[...] = own_src[...]

        def wait():
            other.wait_recv()

            @pl.when(off_diagonal)
            def _():
                same.wait()

        return wait

    def swapped(src, dst):
        made = copy(src, dst, xy_dev)

        @pl.when(x != y)
        def _():
            made.start()

        @pl.when(x == y)
        def _():
            dst[...] = src[...]

        def wait():
            @pl.when(x != y)
            def _():
                made.wait()

        return wait

    class Gather:
        def __init__(self, half, me, right, left, first=None):
            self.half, self.me, self.right, self.left = half, me, right, left
            src = dst = functools.partial(half, me)
            if first is not None:
                src, dst, right, left = first
            self.right0 = send(src(0), dst(0), right)
            self.left1 = send(src(1), dst(1), left)
            self.right1 = send(src(1), dst(1), right)
            self.left0 = send(src(0), dst(0), left)

        def forward(self):
            self.right0.wait_recv()
            half = self.half(plus(self.me, 3), 0)
            self.on_right = send(half, half, self.right)
            self.left1.wait_recv()
            half = self.half(plus(self.me, 1), 1)
            self.on_left = send(half, half, self.left)

        def neighbours(self):
            self.right1.wait_recv()
            self.left0.wait_recv()

        def finish(self):
            self.on_right.wait_recv()
            self.on_left.wait_recv()

    class Reduce:
        def __init__(self, half, tr, arrived, me, right, left, last=None):
            self.half, self.tr, self.arrived, self.me = half, tr, arrived, me
            last_right, last_left = (right, left) if last is None else last
            self.right, self.left = last_right, last_left
            opposite = plus(me, 2)
            self.t0 = send(half(opposite, 0), tr(0), right)
            self.t1 = send(half(opposite, 1), tr(1), left)
            self.r1 = send(half(plus(me, 1), 1), arrived(0, 1), last_right)
            self.l0 = send(half(plus(me, 3), 0), arrived(1, 0), last_left)

        def forward(self):
            self.t0.wait_recv()
            term = self.half(plus(self.me, 1), 0)
            term[...] = (term[...].astype(F32) + self.tr(0)[...].astype(F32)).astype(BF16)
            self.r0 = send(term, self.arrived(0, 0), self.right)
            self.t1.wait_recv()
            term = self.half(plus(self.me, 3), 1)
            term[...] = (term[...].astype(F32) + self.tr(1)[...].astype(F32)).astype(BF16)
            self.l1 = send(term, self.arrived(1, 1), self.left)

        def finish(self, h, own=None):
            own = self.half(self.me, h) if own is None else own
            (self.r0 if h == 0 else self.r1).wait_recv()
            (self.l0 if h == 0 else self.l1).wait_recv()
            return (
                own[...].astype(F32)
                + self.arrived(0, h)[...].astype(F32)
                + self.arrived(1, h)[...].astype(F32)
            )

    def cot_half(k):
        return cot.at[:, pl.ds(pl.multiple_of(k * 256, 256), 256)]

    w_y = Gather(lambda o, h: wt.at[o, pl.ds(h * 128, 128)], y, y_dev[1], y_dev[3])

    key_rows, value_rows = keys[...], values[...]
    starts = jnp.broadcast_to(starts_ref[...] - dp * 128, (128, 128)).T
    row = lax.broadcasted_iota(jnp.int32, (128, 128), 0)
    col = lax.broadcasted_iota(jnp.int32, (128, 128), 1)
    allowed = (col >= starts) & (col <= row)
    for head in range(2):
        scores = lax.dot_general(
            queries[:, head * HD : (head + 1) * HD],
            key_rows,
            (((1,), (1,)), ((), ())),
            preferred_element_type=F32,
        ) / math.sqrt(HD)
        scores = jnp.where(allowed, scores, -1e30)
        top = jnp.max(scores, axis=-1, keepdims=True)
        weights = jnp.where(allowed, jnp.exp(scores - top), 0.0)
        probs = (weights / jnp.sum(weights, axis=-1, keepdims=True)).astype(BF16)
        mine[:, head * HD : (head + 1) * HD] = jnp.dot(
            probs, value_rows, preferred_element_type=F32
        ).astype(BF16)

    def rows64(h):
        return pl.ds(h * 64, 64)

    def ho_x(g):
        return Gather(lambda o, h: ho.at[g, o, c, rows64(h)], x, x_dev[1], x_dev[3])

    def ho_core(g):
        return send(ho.at[g, :, c], ho.at[g, :, c], sibling)

    z_base = used[0]
    used[0] += 4

    def z_copy(k, src):
        return pltpu.make_async_remote_copy(
            src_ref=src,
            dst_ref=z_in.at[k],
            send_sem=ssem.at[z_base + k],
            recv_sem=rsem.at[z_base + k],
            device_id=dev(zh, x, c, plus(zl, k), y),
            device_id_type=MESH,
        )

    def project(g):
        part = jnp.dot(ho[g, 0].reshape(256, 256), wt[0], preferred_element_type=F32)
        for i in range(1, 4):
            part = part + jnp.dot(
                ho[g, i].reshape(256, 256), wt[i], preferred_element_type=F32
            )
        s_y[g] = part.astype(BF16).reshape(2, 128, 256)
        k = plus(g, 4 - zl)

        @pl.when(k != 0)
        def _():
            z_copy(k, s_y.at[g]).start()

    def heads_grad(g):
        def tile(i, carry):
            gp[g, i] = (
                lax.dot_general(
                    ct[g].reshape(256, 256),
                    wt[i],
                    (((1,), (1,)), ((), ())),
                    preferred_element_type=F32,
                )
                .astype(BF16)
                .reshape(2, 128, 256)
            )
            return carry

        lax.fori_loop(0, 4, tile, 0)
        return send(gp.at[g, :, 1 - c], g_in.at[g], sibling)

    def heads_x(g, from_core):
        from_core.wait_recv()

        def tile(i, carry):
            gs[g, i] = (gp[g, i, c].astype(F32) + g_in[g, i].astype(F32)).astype(BF16)
            return carry

        lax.fori_loop(0, 4, tile, 0)
        return Reduce(
            lambda o, h: gs.at[g, o, rows64(h)],
            lambda h: gx_tr.at[g, h],
            lambda side, h: gx_in.at[g, side, rows64(h)],
            x,
            x_dev[1],
            x_dev[3],
        )

    ho_z = Gather(
        lambda o, h: ho.at[o, x, c, rows64(h)],
        zh,
        zh_dev[1],
        zh_dev[3],
        (
            lambda h: mine.at[rows64(h)],
            lambda h: ho.at[zh, y, c, rows64(h)],
            xy_zh_dev[1],
            xy_zh_dev[3],
        ),
    )
    mine_wait = swapped(mine, ho.at[zh, y, c])
    cot_wait = transposed(cot_half(c), cot_half(1 - c), ct.at[zh, c])
    groups = [zh, plus(zh, 3), plus(zh, 1), plus(zh, 2)]
    cgroups = [zl, plus(zl, 3), plus(zl, 2), plus(zl, 1)]
    w_y.forward()
    mine_wait()
    hx = [ho_x(groups[0])]
    ho_z.forward()
    hx[0].forward()
    w_y.neighbours()
    w_y.finish()
    ho_z.neighbours()
    hx.append(ho_x(groups[1]))
    hx.append(ho_x(groups[2]))
    cot_wait()
    ct_zl = [send(ct.at[zl], ct.at[zl], zl_dev[k]) for k in (1, 2, 3)]
    gc = [heads_grad(cgroups[0])]
    hx[0].neighbours()
    hx[0].finish()
    hc = [ho_core(groups[0])]
    gx = [heads_x(cgroups[0], gc[0])]
    hc[0].wait_recv()
    project(groups[0])
    hx[1].forward()
    hx[2].forward()
    ho_z.finish()
    last = ho.at[groups[3], x, c]
    hx_last = [send(last, last, x_dev[k]) for k in (1, 3, 2)]
    for k in (1, 2):
        hx[k].neighbours()
        hx[k].finish()
        hc.append(ho_core(groups[k]))
    for k in (1, 2, 3):
        ct_zl[k - 1].wait_recv()
        gc.append(heads_grad(cgroups[k]))
        if k < 3:
            hc[k].wait_recv()
            project(groups[k])
    for k in (1, 2, 3):
        gx.append(heads_x(cgroups[k], gc[k]))
    gx[0].forward()
    for made in hx_last:
        made.wait_recv()
    hc.append(ho_core(groups[3]))
    hc[3].wait_recv()
    project(groups[3])
    for k in (1, 2, 3):
        gx[k].forward()
    for k in range(4):
        for h in range(2):
            gh[cgroups[k], rows64(h)] = gx[k].finish(h).astype(BF16)
    gz = Reduce(
        lambda o, h: gh.at[o, rows64(h)],
        lambda h: gz_tr.at[h],
        lambda side, h: gz_in.at[side, rows64(h)],
        zh,
        zh_dev[1],
        zh_dev[3],
        (xy_zh_dev[1], xy_zh_dev[3]),
    )
    own_wait = swapped(gh.at[zh], g_own)

    for k in (1, 2, 3):
        z_copy(k, s_y.at[0]).wait_recv()
    for h in range(2):
        q_sum[h] = (
            s_y[zl, h].astype(F32)
            + z_in[1, h].astype(F32)
            + z_in[2, h].astype(F32)
            + z_in[3, h].astype(F32)
        ).astype(BF16)
    p_wait = transposed(q_sum.at[c], q_sum.at[1 - c], t_in.at[c])

    gz.forward()

    def weight_tile(i, carry):
        part = jnp.zeros((256, 256), F32)
        for g in range(4):
            part = part + lax.dot_general(
                ho[g, i].reshape(256, 256),
                ct[g].reshape(256, 256),
                (((0,), (0,)), ((), ())),
                preferred_element_type=F32,
            )
        gw[i] = part.astype(BF16)
        return carry

    lax.fori_loop(0, 4, weight_tile, 0)
    gw_y = Reduce(
        lambda o, h: gw.at[o, pl.ds(h * 128, 128)],
        lambda h: gw_tr.at[h],
        lambda side, h: gw_in.at[side, pl.ds(h * 128, 128)],
        y,
        y_dev[1],
        y_dev[3],
    )
    gw_y.forward()

    p_wait()
    squares = jnp.zeros((128, 1), F32)
    for k in range(2):
        cols = slice(k * 256, (k + 1) * 256)
        part = residual[:, cols].astype(F32) + t_in[k].astype(F32)
        stream[:, cols] = part
        mixed[:, cols] = part.astype(BF16)
        squares = squares + jnp.sum(part * part, axis=1, keepdims=True)
    sq[0] = jnp.broadcast_to(squares, (128, 128)).T[:8]
    norms = [send(sq.at[0], sq.at[k], row_dev[k]) for k in range(1, 16)]

    for h in range(2):
        grad_weight[h * 128 : (h + 1) * 128, :] = gw_y.finish(h).astype(BF16)
    own_wait()
    for h in range(2):
        rows = g_own.at[rows64(h)]
        grad_heads[h * 64 : (h + 1) * 64, :] = gz.finish(h, rows).astype(BF16)

    for made in norms:
        made.wait_recv()
    total = jnp.sum(sq[...], axis=0)
    mean_square = jnp.broadcast_to(total[:1], (128, 128)).T[:, :1] / D_MODEL
    factor = lax.rsqrt(mean_square + EPS)
    for k in range(4):
        cols = slice(k * 128, (k + 1) * 128)
        normed[:, cols] = (stream[:, cols] * factor * gain[k : k + 1, :].astype(F32)).astype(BF16)

    for made in sent:
        made.wait_send()
    for k in (1, 2, 3):
        z_copy(k, s_y.at[0]).wait_send()


def copy_results(*refs):
    sources, results, held = refs[:4], refs[4:8], refs[8:12]
    in_sem, out_sem = refs[12:]
    loads = [pltpu.make_async_copy(sources[k], held[k], in_sem.at[k]) for k in range(4)]
    stores = [pltpu.make_async_copy(held[k], results[k], out_sem.at[k]) for k in range(4)]
    for load in loads:
        load.start()
    for load, store in zip(loads, stores):
        load.wait()
        store.start()
    for store in stores:
        store.wait()


def body(queries, keys, values, doc_start, out_weight, residual, gain, cotangent):
    vmem = pl.BlockSpec(memory_space=pltpu.VMEM)

    def buf(*shape):
        return pltpu.VMEM(shape, BF16)

    sizes = ((128, 512), (128, 512), (256, 256), (128, 256))
    shapes = tuple(jax.ShapeDtypeStruct(size, BF16) for size in sizes)
    results = pl.pallas_call(
        kernel,
        out_shape=shapes,
        in_specs=[pl.BlockSpec(memory_space=pltpu.HBM)] * 8,
        out_specs=(vmem,) * 4,
        scratch_shapes=[
            buf(128, 256),
            buf(4, 4, 2, 128, 256),
            buf(4, 2, 128, 256),
            buf(4, 256, 256),
            buf(4, 2, 128, 256),
            buf(4, 2, 128, 256),
            buf(2, 128, 256),
            buf(2, 128, 256),
            buf(4, 256, 256),
            buf(2, 128, 256),
            buf(2, 256, 256),
            buf(4, 4, 2, 128, 256),
            buf(4, 4, 128, 256),
            buf(4, 4, 128, 256),
            buf(4, 2, 64, 256),
            buf(4, 2, 128, 256),
            buf(4, 128, 256),
            buf(2, 64, 256),
            buf(2, 128, 256),
            buf(128, 256),
            pltpu.VMEM((128, 512), F32),
            pltpu.VMEM((16, 8, 128), F32),
            buf(128, 256),
            buf(128, 128),
            buf(128, 128),
            pltpu.VMEM((1, 128), jnp.int32),
            buf(128, 512),
            buf(4, 128),
            buf(128, 512),
            pltpu.SemaphoreType.DMA((N_COPIES,)),
            pltpu.SemaphoreType.DMA((N_COPIES,)),
            pltpu.SemaphoreType.DMA((N_LOADS,)),
        ],
        compiler_params=pltpu.CompilerParams(
            collective_id=0, has_side_effects=True, vmem_limit_bytes=63 * 2**20
        ),
    )(
        queries,
        keys,
        values,
        doc_start.reshape(1, 128),
        out_weight,
        residual,
        gain.reshape(4, 128),
        cotangent,
    )
    hbm = pl.BlockSpec(memory_space=pltpu.HBM)
    return pl.pallas_call(
        copy_results,
        out_shape=shapes,
        in_specs=[hbm] * 4,
        out_specs=(hbm,) * 4,
        scratch_shapes=[
            *(buf(*size) for size in sizes),
            pltpu.SemaphoreType.DMA((4,)),
            pltpu.SemaphoreType.DMA((4,)),
        ],
        compiler_params=pltpu.CompilerParams(vmem_limit_bytes=63 * 2**20),
    )(*results)


def solution(mesh):
    placed = (
        P("dp", "tensor"),
        P("dp", None),
        P("dp", None),
        P("dp"),
        P("tensor", "dp"),
        P("dp", "tensor"),
        P("tensor"),
        P("dp", "tensor"),
    )
    return jax.shard_map(
        body,
        mesh=mesh,
        in_specs=placed,
        out_specs=(P("dp", "tensor"), P("dp", "tensor"), P("tensor", "dp"), P("dp", "tensor")),
        check_vma=False,
    )
```
